256 devices in a mesh: vrow: 32 (over z_hi, y, core), vcol: 8 (over x, z_lo).
Axes of the slice: x: 4, y: 4, z: 8 (z_hi: 4, z_lo: 2; z = z_hi * 2 + z_lo), core: 2. Of those that a mesh axis runs over, the one named last changes fastest.
Arguments:
- pairs: int32 [64, 2], replicated, may hold values from 0 to 119, as said below
- offsets: int32 [2, 2], replicated, may hold values from 0 to 1016, as said below
- amplitudes: bfloat16 [64, 1024, 1024], P(None, 'vrow', 'vcol'), may hold values from -0.59765625 to 0.59765625
- slabs: bfloat16 [2, 2, 1024, 8, 2304], P(None, None, ('vrow', 'vcol')), may hold values from -0.86328125 to 0.86328125
Outputs:
- residual: float32 [64, 1024, 1024], P(None, 'vrow', 'vcol')
The draws below stay inside these ranges and needn't reach their ends.
Inputs may be any that keep to these rules, and one draw needn't show every extreme that they name: `pairs`: each row is an occupied pair i <= j; some rows have i = j. `offsets`: every offset is a multiple of 8.
All inputs are finite; a program needn't handle non-finite values.
Results may differ from the reference program's by a relative error of at most 0.0003.
Values may be sent and summed in bfloat16 or wider, within the bound.
No kernel may reach another device: no remote copies, remote signals or barrier semaphores. Data moves between devices by JAX's collectives and lax.ppermute only.
A program may use at most 128 MiB of HBM per device.

```python
import jax
import jax.numpy as jnp
from jax import lax

NOCC = 120
V = 1024
Q = 2304
BLK = 8
P_SIZE = 64
STEPS = 2


def draw_pairs(key, part):
    key = jax.random.fold_in(key, 11)
    key_first, key_span, key_diag = jax.random.split(key, 3)
    first = jax.random.randint(key_first, (P_SIZE,), 0, NOCC)
    span = jax.random.randint(key_span, (P_SIZE,), 0, NOCC)
    second = first + jnp.remainder(span, NOCC - first)
    flag = jax.random.randint(key_diag, (P_SIZE,), 0, 4) == 0
    second = jnp.where(flag, first, second)
    first = first.at[0].set(0)
    second = second.at[0].set(NOCC - 1)
    second = second.at[1].set(first[1])
    return jnp.stack([first, second], axis=1).astype(jnp.int32)


def draw_offsets(key, part):
    key = jax.random.fold_in(key, 23)
    key_picks, key_place = jax.random.split(key, 2)
    picks = jax.random.randint(key_picks, (STEPS * 2,), 0, V // BLK)
    place = jax.random.randint(key_place, (), 0, STEPS * 2)
    slots = jnp.arange(STEPS * 2)
    picks = jnp.where(slots == place, V // BLK - 1, picks)
    return (picks * BLK).reshape(STEPS, 2).astype(jnp.int32)


def levels(rng, dims, shards, low, largest):
    def one(position, shards_of):
        heights = jax.random.uniform(jax.random.fold_in(jax.random.fold_in(rng, 6), position), (shards_of,), jnp.float32, low / len(shards), largest / len(shards))
        return jnp.repeat(jnp.exp(heights), dims[position] // shards_of).reshape((-1,) + (1,) * (len(dims) - position - 1))

    level = one(*shards[0])
    for cut in shards[1:]:
        level = level * one(*cut)
    return level


def scatter_about(stream_key, shape, scale, reach, cuts=(), held_as=jnp.bfloat16):
    values = jax.random.normal(stream_key, shape, jnp.float32) * scale
    if len(cuts) > 0:
        values = levels(stream_key, shape, cuts, -0.22, 0.18) * values
    return jnp.clip(values, min=-reach, max=reach).astype(held_as)


def setup_inputs(seed: int = 0) -> dict:
    keys = jax.random.split(jax.random.key(seed), 5)
    return {
        "pairs": draw_pairs(jax.random.fold_in(keys[4], 71), 0),
        "offsets": draw_offsets(jax.random.fold_in(keys[4], 71), 0),
        "amplitudes": scatter_about(keys[2], (P_SIZE, V, V), 0.1, 0.59765625, ((1, 32), (2, 8))),
        "slabs": scatter_about(keys[3], (STEPS, 2, V, BLK, Q), (Q ** -0.25), 0.86328125, ((2, 256),)),
    }


def reference(pairs, offsets, amplitudes, slabs):
    offdiag = (pairs[:, 0] != pairs[:, 1]).astype(jnp.float32)
    amp = amplitudes.astype(jnp.float32)
    zero = jnp.zeros((), jnp.int32)
    total = jnp.zeros((P_SIZE, V, V), jnp.float32)
    starts = (jnp.arange(V // 128) * 128).astype(jnp.int32)
    for k in range(STEPS):
        first = offsets[k, 0].astype(jnp.int32)
        second = offsets[k, 1].astype(jnp.int32)
        forward = lax.dynamic_slice(amp, (zero, first, second), (P_SIZE, BLK, BLK))
        mirror = jnp.transpose(lax.dynamic_slice(amp, (zero, second, first), (P_SIZE, BLK, BLK)), (0, 2, 1))
        plus = 0.5 * (forward + mirror)
        minus = 0.5 * (forward - mirror) * offdiag[:, None, None]
        upper = plus + minus
        lower = plus - minus
        cols_c = slabs[k, 0].reshape(V * BLK, Q)
        cols_d = slabs[k, 1].reshape(V * BLK, Q)

        def block(start):
            rows_c = lax.dynamic_slice_in_dim(slabs[k, 0], start, 128, 0).reshape(128 * BLK, Q)
            rows_d = lax.dynamic_slice_in_dim(slabs[k, 1], start, 128, 0).reshape(128 * BLK, Q)
            direct = lax.dot_general(rows_c, cols_d, (((1,), (1,)), ((), ())), preferred_element_type=jnp.float32).reshape(128, BLK, V, BLK)
            swapped = lax.dot_general(rows_d, cols_c, (((1,), (1,)), ((), ())), preferred_element_type=jnp.float32).reshape(128, BLK, V, BLK)
            term = jnp.einsum("acbd,pcd->pab", direct, upper, precision=lax.Precision.HIGHEST)
            return term + jnp.einsum("adbc,pcd->pab", swapped, lower, precision=lax.Precision.HIGHEST)

        parts = lax.map(block, starts)
        total = total + jnp.transpose(parts, (1, 0, 2, 3)).reshape(P_SIZE, V, V)
    return total
```

```python
import jax
import jax.numpy as jnp
import numpy as np
from jax import lax
from jax.experimental import pallas as pl
from jax.experimental.pallas import tpu as pltpu
from jax.sharding import PartitionSpec as P

BLK = 8
P_SIZE = 64
STEPS = 2
AXES = ("vrow", "vcol")
X, Y, Z, CORES = 4, 4, 8, 2
DEPTH = 2304
OWN = 4


SMEM = pl.BlockSpec(memory_space=pltpu.SMEM)
VMEM = pl.BlockSpec(memory_space=pltpu.VMEM)
HBM = pl.BlockSpec(memory_space=pl.ANY)


def coords(me):
    return me >> 1 & 3, me >> 4 & 3, me >> 6 << 1 | me & 1, me >> 3 & 1


def flat(x, y, z, c):
    x, y, z, c = x % X, y % Y, z % Z, c % CORES
    return z // 2 << 6 | y << 4 | c << 3 | x << 1 | z % 2


def send(block, where):
    pairs = []
    for me in range(X * Y * Z * CORES):
        pairs.append((me, flat(*where(*coords(me)))))
    return lax.ppermute(block, AXES, pairs)


def rehome(x, y, z, c):
    return x, z % 2 * 2 + y % 2, z // 2 * 2 + y // 2, c


def blocks_kernel(me, offsets, amplitudes, _, out, window, sem):
    out[...] = jnp.zeros_like(out)
    for j in range(2 * STEPS):
        first, second = offsets[j // 2, j % 2], offsets[j // 2, 1 - j % 2]
        row, at_lane = first & 31, second & 127

        @pl.when(me[0] == (first >> 5 << 3 | second >> 7))
        def _(j=j, row=row, at_lane=at_lane):
            rows = pl.ds(pl.multiple_of(row & 16, 16), 16)
            copy = pltpu.make_async_copy(amplitudes.at[:, rows, :], window, sem)
            copy.start()
            copy.wait()
            block = window[...].astype(jnp.float32)
            block = jnp.where(row & 8 == 0, block[:, :8], block[:, 8:])
            lane = lax.broadcasted_iota(jnp.int32, (P_SIZE, 128), 1)
            total = jnp.zeros((P_SIZE, 128), jnp.float32)
            for r in range(BLK):
                line = jnp.where((lane >= at_lane) & (lane < at_lane + BLK), block[:, r], 0.0)
                shift = (128 + j % 2 * 64 + r * BLK - at_lane) & 127
                total = total + pltpu.roll(line, shift, 1)
            total = total.astype(jnp.bfloat16)
            for n in range(4):
                at = 128 * (j // 2 * 4 + n)
                out[:, at : at + 128] += total[16 * n : 16 * n + 16]


def own_blocks(me, offsets, amplitudes, rows):
    return pl.pallas_call(
        blocks_kernel,
        out_shape=jax.ShapeDtypeStruct((16, 1024), jnp.bfloat16),
        in_specs=[SMEM, SMEM, HBM, HBM],
        out_specs=VMEM,
        scratch_shapes=[
            pltpu.VMEM((P_SIZE, 16, 128), jnp.bfloat16),
            pltpu.SemaphoreType.DMA(()),
        ],
        compiler_params=pltpu.CompilerParams(vmem_limit_bytes=4 << 20),
        name="blocks",
    )(me, offsets, amplitudes, rows)


def one_hot(to, dtype):
    lane = lax.broadcasted_iota(jnp.int32, (128, 128), 0)
    return jnp.where(to(lane) == lax.broadcasted_iota(jnp.int32, (128, 128), 1), 1.0, 0.0).astype(
        dtype
    )


def ladder_kernel(me, offdiag, swap, a_in, *refs):
    b_in = refs[0:4]
    keep, give = refs[4:6]
    a_all, b_all, m_all, tail, sems = refs[6:]
    x, y, z, c = coords(me[0])
    copies = []
    for j in range(8):
        at = (((j // 2 - (z >> 1)) & 3) * 2 + j % 2) * 64
        copies.append(
            pltpu.make_async_copy(
                a_in.at[pl.ds(64 * j, 64), :],
                a_all.at[pl.ds(pl.multiple_of(at, 64), 64), :],
                sems.at[j],
            )
        )
    for d in range(BLK):
        for j in range(4):
            copies.append(
                pltpu.make_async_copy(
                    b_in[j].at[pl.ds(32 * d, 32), :],
                    b_all.at[d, pl.ds(32 * j, 32), :],
                    sems.at[8 + d * 4 + j],
                )
            )
    for j in range(4):
        copies.append(
            pltpu.make_async_copy(
                b_in[j].at[pl.ds(256, 16), pl.ds(0, 1024)], tail.at[j], sems.at[40 + j]
            )
        )
    for copy in copies:
        copy.start()
    for copy in copies[:8]:
        copy.wait()
    for d in range(0, BLK, 2):
        for copy in copies[8 + 4 * d : 16 + 4 * d]:
            copy.wait()
        cols = b_all[d : d + 2].reshape(256, DEPTH)
        m = lax.dot_general(
            a_all[...], cols, (((1,), (1,)), ((), ())), preferred_element_type=jnp.float32
        )
        m_all[:, d] = m[:, :128].reshape(64, BLK, 128)
        m_all[:, d + 1] = m[:, 128:].reshape(64, BLK, 128)
    for copy in copies[40:]:
        copy.wait()
    t = tail[...].astype(jnp.float32)
    t = t[0] + t[1] + t[2] + t[3]
    parts = []
    for n in range(4):
        parts.append(
            jnp.where(c == 0, t[:, 128 * n : 128 * n + 128], t[:, 128 * n + 512 : 128 * n + 640])
        )
    t = jnp.concatenate(parts).astype(jnp.bfloat16)
    t = jnp.dot(t, swap[...], preferred_element_type=jnp.float32)
    forward, mirror = t[:, :64], t[:, 64:]
    plus = 0.5 * (forward + mirror)
    minus = 0.5 * (forward - mirror) * offdiag[:, :64]
    u = jnp.concatenate([plus + minus, plus - minus])
    hi = u.astype(jnp.bfloat16)
    lo = (u - hi.astype(jnp.float32)).astype(jnp.bfloat16)
    left = jnp.concatenate([hi, hi, lo], axis=1)

    def target(lane):
        near, far = lane >> 3 & 3, lane >> 5
        src_x = (x - jnp.where(c == 0, near, far)) & 3
        src_y = (y - jnp.where(c == 0, far, near)) & 3
        return (
            (src_y >> 1) * 64
            + ((src_y ^ y) & 1) * 32
            + ((lane >> 2 ^ c) & 1) * 16
            + src_x * 4
            + (lane & 3)
        )

    order = one_hot(target, jnp.bfloat16)
    for g in range(32):
        w = m_all[2 * g : 2 * g + 2].reshape(128, 128)
        hi = w.astype(jnp.bfloat16)
        lo = (w - hi.astype(jnp.float32)).astype(jnp.bfloat16)
        both = jnp.dot(
            jnp.concatenate([hi, lo]), order, preferred_element_type=jnp.float32
        ).astype(jnp.bfloat16)
        parts = []
        for n in range(2):
            hi, lo = both[64 * n : 64 * n + 64], both[128 + 64 * n : 192 + 64 * n]
            parts.append(jnp.concatenate([hi, lo, hi]))
        res = jnp.dot(left, jnp.concatenate(parts, axis=1), preferred_element_type=jnp.float32)
        kz, zl, ec, i = g // 8, g // 4 % 2, g // 2 % 2, g % 2 * 2
        at = 8 * ((1 - c) if ec else c) + 4 * zl + i
        x0, x1 = res[64:, :128], res[64:, 128:]
        top = jnp.concatenate([x0[:, :64], x1[:, :64]], axis=1)
        bottom = jnp.concatenate([x0[:, 64:], x1[:, 64:]], axis=1)
        turned = jnp.concatenate([top, bottom]).T
        kx = (kz + (z >> 1) - x) & 3
        for n in range(2):
            one = res[:64, 128 * n : 128 * n + 128].reshape(4, 16, 128)
            two = turned[64 * n : 64 * n + 64].reshape(4, 16, 128)
            keep[jnp.where(c == 0, kz, kx), at + n] = jnp.where(c == 0, one, two)
            give[jnp.where(c == 0, kx, kz), at + n] = jnp.where(c == 0, two, one)


def ladder(me, offdiag, swap, rows, cols):
    f32, bf16 = jnp.float32, jnp.bfloat16
    return pl.pallas_call(
        ladder_kernel,
        out_shape=[jax.ShapeDtypeStruct((4, 16, 4, 16, 128), f32)] * 2,
        in_specs=[SMEM, VMEM, VMEM] + [HBM] * 5,
        out_specs=[VMEM] * 2,
        scratch_shapes=[
            pltpu.VMEM((512, DEPTH), bf16),
            pltpu.VMEM((BLK, 128, DEPTH), bf16),
            pltpu.VMEM((64, BLK, BLK, 128), f32),
            pltpu.VMEM((4, 16, 1024), bf16),
            pltpu.SemaphoreType.DMA((44,)),
        ],
        compiler_params=pltpu.CompilerParams(vmem_limit_bytes=20 << 20),
        name="ladder",
    )(me, offdiag, swap, rows, *cols)


def route_kernel(me, *refs):
    got, out = refs[:4], refs[4:8]
    x, _, z, c = coords(me[0])
    for shift in range(4):

        @pl.when((c == 0) & ((((z >> 1) - x) & 3) == shift))
        def _(shift=shift):
            for j in range(4):
                out[j][...] = got[(shift - j) % 4][...]

    @pl.when(c == 1)
    def _():
        for e in range(2):
            for k in range(4):
                at = 2 * (k % 2)
                out[2 * e + k // 2][:, at : at + 2] = got[k][:, 2 * e : 2 * e + 2]


def route(me, got):
    return pl.pallas_call(
        route_kernel,
        out_shape=[jax.ShapeDtypeStruct(got[0].shape, got[0].dtype)] * 4,
        in_specs=[SMEM] + [VMEM] * 4,
        out_specs=[VMEM] * 4,
        compiler_params=pltpu.CompilerParams(vmem_limit_bytes=10 << 20),
        name="route",
    )(me, *got)


def split_kernel(me, *refs):
    own, out = refs[:4], refs[4]
    c = coords(me[0])[3]

    @pl.when(c == 0)
    def _():
        for j in range(4):
            out[j] = own[j][8:]

    @pl.when(c == 1)
    def _():
        for j in range(4):
            for a5 in range(2):
                for k in range(2):
                    out[j, :, 2 * a5 + k] = own[j][8 * a5 : 8 * a5 + 8, 2 * k]


def split(me, own):
    return pl.pallas_call(
        split_kernel,
        out_shape=jax.ShapeDtypeStruct((4, 8, 4, 16, 128), own[0].dtype),
        in_specs=[SMEM] + [VMEM] * 4,
        out_specs=VMEM,
        compiler_params=pltpu.CompilerParams(vmem_limit_bytes=10 << 20),
        name="split",
    )(me, *own)


def finish_kernel(me, *refs):
    own, other, out = refs[:4], refs[4], refs[5]
    r1, r2 = refs[6:]
    x, y, _, c = coords(me[0])

    def fetch(core):
        for j in range(4):
            r1[(x - j) & 3] = other[j] if core else own[j][:8]
            for a5 in range(2):
                for k in range(2):
                    if core:
                        block = own[j][8 * a5 : 8 * a5 + 8, 2 * k + 1]
                    else:
                        block = other[j, :, 2 * a5 + k]
                    r2[(y & 1) ^ (j // 2), a5, (x - 2 * (j % 2) - k) & 3] = block

    for core in range(2):

        @pl.when(c == core)
        def _(core=core):
            fetch(core)

    order = one_hot(
        lambda lane: ((lane >> 5 ^ y) & 1) * 64
        + (lane >> 4 & 1) * 32
        + (lane >> 2 & 3) * 8
        + (lane >> 6) * 4
        + (lane & 3),
        jnp.float32,
    )
    for g in range(4):
        t = jnp.dot(
            r1[g].reshape(8 * P_SIZE, 128),
            order,
            preferred_element_type=jnp.float32,
            precision=lax.Precision.HIGHEST,
        )
        for n in range(8):
            out[:, 8 * g + n, :] = t[64 * n : 64 * n + 64]
    for r in range(16):
        t = r2[:, :, :, :, r, :].reshape(128, 128).T
        for b2 in range(2):
            row = r // 4 * 8 + b2 * 4 + r % 4
            out[:, row, :] = out[:, row, :] + t[64 * b2 : 64 * b2 + 64]


def finish(me, own, other):
    f32 = jnp.float32
    return pl.pallas_call(
        finish_kernel,
        out_shape=jax.ShapeDtypeStruct((P_SIZE, 32, 128), f32),
        in_specs=[SMEM] + [VMEM] * 5,
        out_specs=VMEM,
        scratch_shapes=[
            pltpu.VMEM((4, 8, 4, 16, 128), f32),
            pltpu.VMEM((2, 2, 4, 8, 16, 128), f32),
        ],
        compiler_params=pltpu.CompilerParams(vmem_limit_bytes=16 << 20),
        name="finish",
    )(me, *own, other)


def transposed_forward():
    m = np.zeros((128, 128), np.float32)
    for c in range(BLK):
        for d in range(BLK):
            m[c * BLK + d, d * BLK + c] = 1
            m[64 + d * BLK + c, 64 + d * BLK + c] = 1
    return m


def on_device(pairs, offsets, amplitudes, slabs):
    me = lax.axis_index(AXES)
    c = me >> 3 & 1
    core = lambda x, y, z, c: (x, y, z, c + 1)
    slabs = slabs.reshape(STEPS, 2, OWN * BLK, DEPTH)
    mine = lax.dynamic_index_in_dim(slabs, c, 0, keepdims=False)
    yours = lax.dynamic_index_in_dim(slabs, 1 - c, 0, keepdims=False)
    swapped = send(yours[0], core)
    mixed = jnp.concatenate([mine[0], swapped])
    groups = [
        [flat(x, y, z, k) for z in range(Z)]
        for x in range(X)
        for y in range(Y)
        for k in range(CORES)
    ]
    rows = lax.all_gather(mixed, AXES, axis_index_groups=groups, axis=0, tiled=True)
    cols = [
        send(mine[1], rehome),
        send(yours[1], lambda x, y, z, c: rehome(x, y, z, c + 1)),
    ]
    me = me[None]
    t = own_blocks(me, offsets, amplitudes, mixed)
    t = (
        t
        + send(t, core)
        + send(t, lambda x, y, z, c: (x, y, z ^ 1, c))
        + send(t, lambda x, y, z, c: (x, y, z ^ 1, c + 1))
    )

    def near(n):
        return lambda x, y, z, c: (x + n * (1 - c), y + n * c, z, c)

    def far(n):
        return lambda x, y, z, c: (x + n * c, y + n * (1 - c), z, c)

    first = [jnp.concatenate(cols)]
    first += [send(first[0], near(n)) for n in range(1, 4)]
    t = t + cols[0][:16, :1024] * 0 + cols[1][:16, :1024] * 0
    t = t + sum(send(t, lambda x, y, z, c, n=n: (x, y, z ^ n, c)) for n in (2, 4, 6))
    t = t + sum(send(t, near(n)) for n in range(1, 4))
    t = jnp.pad(t, ((0, 0), (0, DEPTH - 1024)))
    cols = jnp.stack([m.reshape(8, BLK, DEPTH) for m in first])
    cols = jnp.transpose(cols, (2, 0, 1, 3)).reshape(256, DEPTH)
    second = [jnp.concatenate([cols, t])]
    second += [send(second[0], far(n)) for n in range(1, 4)]
    offdiag = (pairs[:, 0] != pairs[:, 1]).astype(jnp.float32)
    offdiag = jnp.broadcast_to(offdiag[:, None], (P_SIZE, 128))
    swap = jnp.asarray(transposed_forward(), jnp.bfloat16)
    keep, give = ladder(me, offdiag, swap, rows, second)

    taken = send(give, core)
    got = [keep[0] + taken[0]]
    for k in range(1, 4):
        got.append(
            send(
                keep[k] + taken[k],
                lambda x, y, z, c, k=k: (x + k * c, y, z + 2 * k * (1 - c), c),
            )
        )

    def onward(j):
        def where(x, y, z, c):
            if c == 0:
                return x + j, y, z, c
            x, y, z, c = rehome(x, y, z, c)
            return x, y ^ (j // 2), z, c

        return where

    own = [send(piece, onward(j)) for j, piece in enumerate(route(me, got))]
    return finish(me, own, send(split(me, own), core))


def solution(mesh):
    in_specs = (P(), P(), P(None, "vrow", "vcol"), P(None, None, ("vrow", "vcol"), None, None))
    out_specs = P(None, "vrow", "vcol")
    return jax.shard_map(
        on_device, mesh=mesh, in_specs=in_specs, out_specs=out_specs, check_vma=False
    )
```

```python
import jax
import jax.numpy as jnp
import numpy as np
from jax import lax
from jax.experimental import pallas as pl
from jax.experimental.pallas import tpu as pltpu
from jax.sharding import PartitionSpec as P

BLK = 8
P_SIZE = 64
STEPS = 2
AXES = ("vrow", "vcol")
X, Y, Z, CORES = 4, 4, 8, 2
DEPTH = 2304
OWN = 4


SMEM = pl.BlockSpec(memory_space=pltpu.SMEM)
VMEM = pl.BlockSpec(memory_space=pltpu.VMEM)
HBM = pl.BlockSpec(memory_space=pl.ANY)


def coords(me):
    return me >> 1 & 3, me >> 4 & 3, me >> 6 << 1 | me & 1, me >> 3 & 1


def flat(x, y, z, c):
    x, y, z, c = x % X, y % Y, z % Z, c % CORES
    return z // 2 << 6 | y << 4 | c << 3 | x << 1 | z % 2


def send(block, where):
    pairs = []
    for me in range(X * Y * Z * CORES):
        pairs.append((me, flat(*where(*coords(me)))))
    return lax.ppermute(block, AXES, pairs)


def rehome(x, y, z, c):
    return x, z % 2 * 2 + y % 2, z // 2 * 2 + y // 2, c


def blocks_kernel(me, offsets, amplitudes, _, out, window, sem):
    out[...] = jnp.zeros_like(out)
    for j in range(2 * STEPS):
        first, second = offsets[j // 2, j % 2], offsets[j // 2, 1 - j % 2]
        row, at_lane = first & 31, second & 127

        @pl.when(me[0] == (first >> 5 << 3 | second >> 7))
        def _(j=j, row=row, at_lane=at_lane):
            rows = pl.ds(pl.multiple_of(row & 16, 16), 16)
            copy = pltpu.make_async_copy(amplitudes.at[:, rows, :], window, sem)
            copy.start()
            copy.wait()
            block = window[...].astype(jnp.float32)
            block = jnp.where(row & 8 == 0, block[:, :8], block[:, 8:])
            lane = lax.broadcasted_iota(jnp.int32, (P_SIZE, 128), 1)
            total = jnp.zeros((P_SIZE, 128), jnp.float32)
            for r in range(BLK):
                line = jnp.where((lane >= at_lane) & (lane < at_lane + BLK), block[:, r], 0.0)
                shift = (128 + j % 2 * 64 + r * BLK - at_lane) & 127
                total = total + pltpu.roll(line, shift, 1)
            total = total.astype(jnp.bfloat16)
            for n in range(4):
                at = 128 * (j // 2 * 4 + n)
                out[:, at : at + 128] += total[16 * n : 16 * n + 16]


def own_blocks(me, offsets, amplitudes, rows):
    return pl.pallas_call(
        blocks_kernel,
        out_shape=jax.ShapeDtypeStruct((16, 1024), jnp.bfloat16),
        in_specs=[SMEM, SMEM, HBM, HBM],
        out_specs=VMEM,
        scratch_shapes=[
            pltpu.VMEM((P_SIZE, 16, 128), jnp.bfloat16),
            pltpu.SemaphoreType.DMA(()),
        ],
        compiler_params=pltpu.CompilerParams(vmem_limit_bytes=4 << 20),
        name="blocks",
    )(me, offsets, amplitudes, rows)


def one_hot(to, dtype):
    lane = lax.broadcasted_iota(jnp.int32, (128, 128), 0)
    return jnp.where(to(lane) == lax.broadcasted_iota(jnp.int32, (128, 128), 1), 1.0, 0.0).astype(
        dtype
    )


def ladder_kernel(me, offdiag, swap, a_in, *refs):
    b_in = refs[0:4]
    keep, give = refs[4:6]
    a_all, b_all, m_all, tail, sems = refs[6:]
    x, y, z, c = coords(me[0])
    copies = []
    for j in range(8):
        at = (((j // 2 - (z >> 1)) & 3) * 2 + j % 2) * 64
        copies.append(
            pltpu.make_async_copy(
                a_in.at[pl.ds(64 * j, 64), :],
                a_all.at[pl.ds(pl.multiple_of(at, 64), 64), :],
                sems.at[j],
            )
        )
    for d in range(BLK):
        for j in range(4):
            copies.append(
                pltpu.make_async_copy(
                    b_in[j].at[pl.ds(32 * d, 32), :],
                    b_all.at[d, pl.ds(32 * j, 32), :],
                    sems.at[8 + d * 4 + j],
                )
            )
    for j in range(4):
        copies.append(
            pltpu.make_async_copy(
                b_in[j].at[pl.ds(256, 16), pl.ds(0, 1024)], tail.at[j], sems.at[40 + j]
            )
        )
    for copy in copies:
        copy.start()
    for copy in copies[:8]:
        copy.wait()
    for d in range(0, BLK, 2):
        for copy in copies[8 + 4 * d : 16 + 4 * d]:
            copy.wait()
        cols = b_all[d : d + 2].reshape(256, DEPTH)
        m = lax.dot_general(
            a_all[...], cols, (((1,), (1,)), ((), ())), preferred_element_type=jnp.float32
        )
        m_all[:, d] = m[:, :128].reshape(64, BLK, 128)
        m_all[:, d + 1] = m[:, 128:].reshape(64, BLK, 128)
    for copy in copies[40:]:
        copy.wait()
    t = tail[...].astype(jnp.float32)
    t = t[0] + t[1] + t[2] + t[3]
    parts = []
    for n in range(4):
        parts.append(
            jnp.where(c == 0, t[:, 128 * n : 128 * n + 128], t[:, 128 * n + 512 : 128 * n + 640])
        )
    t = jnp.concatenate(parts).astype(jnp.bfloat16)
    t = jnp.dot(t, swap[...], preferred_element_type=jnp.float32)
    forward, mirror = t[:, :64], t[:, 64:]
    plus = 0.5 * (forward + mirror)
    minus = 0.5 * (forward - mirror) * offdiag[:, :64]
    u = jnp.concatenate([plus + minus, plus - minus])
    hi = u.astype(jnp.bfloat16)
    lo = (u - hi.astype(jnp.float32)).astype(jnp.bfloat16)
    left = jnp.concatenate([hi, hi, lo], axis=1)

    def target(lane):
        near, far = lane >> 3 & 3, lane >> 5
        src_x = (x - jnp.where(c == 0, near, far)) & 3
        src_y = (y - jnp.where(c == 0, far, near)) & 3
        return (
            (src_y >> 1) * 64
            + ((src_y ^ y) & 1) * 32
            + ((lane >> 2 ^ c) & 1) * 16
            + src_x * 4
            + (lane & 3)
        )

    order = one_hot(target, jnp.bfloat16)
    for g in range(32):
        w = m_all[2 * g : 2 * g + 2].reshape(128, 128)
        hi = w.astype(jnp.bfloat16)
        lo = (w - hi.astype(jnp.float32)).astype(jnp.bfloat16)
        both = jnp.dot(
            jnp.concatenate([hi, lo]), order, preferred_element_type=jnp.float32
        ).astype(jnp.bfloat16)
        parts = []
        for n in range(2):
            hi, lo = both[64 * n : 64 * n + 64], both[128 + 64 * n : 192 + 64 * n]
            parts.append(jnp.concatenate([hi, lo, hi]))
        res = jnp.dot(left, jnp.concatenate(parts, axis=1), preferred_element_type=jnp.float32)
        kz, zl, ec, i = g // 8, g // 4 % 2, g // 2 % 2, g % 2 * 2
        at = 8 * ((1 - c) if ec else c) + 4 * zl + i
        x0, x1 = res[64:, :128], res[64:, 128:]
        top = jnp.concatenate([x0[:, :64], x1[:, :64]], axis=1)
        bottom = jnp.concatenate([x0[:, 64:], x1[:, 64:]], axis=1)
        turned = jnp.concatenate([top, bottom]).T
        kx = (kz + (z >> 1) - x) & 3
        for n in range(2):
            one = res[:64, 128 * n : 128 * n + 128].reshape(4, 16, 128)
            two = turned[64 * n : 64 * n + 64].reshape(4, 16, 128)
            keep[jnp.where(c == 0, kz, kx), at + n] = jnp.where(c == 0, one, two)
            give[jnp.where(c == 0, kx, kz), at + n] = jnp.where(c == 0, two, one)


def ladder(me, offdiag, swap, rows, cols):
    f32, bf16 = jnp.float32, jnp.bfloat16
    return pl.pallas_call(
        ladder_kernel,
        out_shape=[jax.ShapeDtypeStruct((4, 16, 4, 16, 128), f32)] * 2,
        in_specs=[SMEM, VMEM, VMEM] + [HBM] * 5,
        out_specs=[VMEM] * 2,
        scratch_shapes=[
            pltpu.VMEM((512, DEPTH), bf16),
            pltpu.VMEM((BLK, 128, DEPTH), bf16),
            pltpu.VMEM((64, BLK, BLK, 128), f32),
            pltpu.VMEM((4, 16, 1024), bf16),
            pltpu.SemaphoreType.DMA((44,)),
        ],
        compiler_params=pltpu.CompilerParams(vmem_limit_bytes=56 << 20),
        name="ladder",
    )(me, offdiag, swap, rows, *cols)


def pack(block):
    top = jnp.max(jnp.abs(block), axis=0, keepdims=True)
    power = jnp.clip(jnp.floor(jnp.log2(top)), -100.0, 100.0)
    return jnp.concatenate([block * jnp.exp2(14.0 - power), power]).astype(jnp.float16)


def unpack(block):
    block = block.astype(jnp.float32)
    return block[:16] * jnp.exp2(block[16:] - 14.0)


def route(me, got):
    x, _, z, c = coords(me)
    every = jnp.stack(got)
    out = []
    for j in range(4):
        whole = lax.dynamic_index_in_dim(every, ((z >> 1) - x - j) & 3, 0, keepdims=False)
        e, k = j // 2, j % 2 * 2
        rows = [got[k + n][:, 2 * e : 2 * e + 2] for n in range(2)]
        out.append(jnp.where(c == 0, whole, jnp.concatenate(rows, axis=1)))
    return out


def split_kernel(me, *refs):
    own, out = refs[:4], refs[4]
    c = coords(me[0])[3]

    @pl.when(c == 0)
    def _():
        for j in range(4):
            out[j] = own[j][8:]

    @pl.when(c == 1)
    def _():
        for j in range(4):
            for a5 in range(2):
                for k in range(2):
                    out[j, :, 2 * a5 + k] = own[j][8 * a5 : 8 * a5 + 8, 2 * k]


def split(me, own):
    return pl.pallas_call(
        split_kernel,
        out_shape=jax.ShapeDtypeStruct((4, 8, 4, 16, 128), own[0].dtype),
        in_specs=[SMEM] + [VMEM] * 4,
        out_specs=VMEM,
        compiler_params=pltpu.CompilerParams(vmem_limit_bytes=10 << 20),
        name="split",
    )(me, *own)


def finish_kernel(me, *refs):
    own, other, out = refs[:4], refs[4], refs[5]
    r1, r2 = refs[6:]
    x, y, _, c = coords(me[0])

    def fetch(core):
        for j in range(4):
            r1[(x - j) & 3] = other[j] if core else own[j][:8]
            for a5 in range(2):
                for k in range(2):
                    if core:
                        block = own[j][8 * a5 : 8 * a5 + 8, 2 * k + 1]
                    else:
                        block = other[j, :, 2 * a5 + k]
                    r2[(y & 1) ^ (j // 2), a5, (x - 2 * (j % 2) - k) & 3] = block

    for core in range(2):

        @pl.when(c == core)
        def _(core=core):
            fetch(core)

    order = one_hot(
        lambda lane: ((lane >> 5 ^ y) & 1) * 64
        + (lane >> 4 & 1) * 32
        + (lane >> 2 & 3) * 8
        + (lane >> 6) * 4
        + (lane & 3),
        jnp.float32,
    )
    for g in range(4):
        t = jnp.dot(
            r1[g].reshape(8 * P_SIZE, 128),
            order,
            preferred_element_type=jnp.float32,
            precision=lax.Precision.HIGHEST,
        )
        for n in range(8):
            out[:, 8 * g + n, :] = t[64 * n : 64 * n + 64]
    for r in range(16):
        t = r2[:, :, :, :, r, :].reshape(128, 128).T
        for b2 in range(2):
            row = r // 4 * 8 + b2 * 4 + r % 4
            out[:, row, :] = out[:, row, :] + t[64 * b2 : 64 * b2 + 64]


def finish(me, own, other):
    f32 = jnp.float32
    return pl.pallas_call(
        finish_kernel,
        out_shape=jax.ShapeDtypeStruct((P_SIZE, 32, 128), f32),
        in_specs=[SMEM] + [VMEM] * 5,
        out_specs=VMEM,
        scratch_shapes=[
            pltpu.VMEM((4, 8, 4, 16, 128), f32),
            pltpu.VMEM((2, 2, 4, 8, 16, 128), f32),
        ],
        compiler_params=pltpu.CompilerParams(vmem_limit_bytes=16 << 20),
        name="finish",
    )(me, *own, other)


def transposed_forward():
    m = np.zeros((128, 128), np.float32)
    for c in range(BLK):
        for d in range(BLK):
            m[c * BLK + d, d * BLK + c] = 1
            m[64 + d * BLK + c, 64 + d * BLK + c] = 1
    return m


def on_device(pairs, offsets, amplitudes, slabs):
    me = lax.axis_index(AXES)
    c = me >> 3 & 1
    core = lambda x, y, z, c: (x, y, z, c + 1)
    slabs = slabs.reshape(STEPS, 2, OWN * BLK, DEPTH)
    mine = lax.dynamic_index_in_dim(slabs, c, 0, keepdims=False)
    yours = lax.dynamic_index_in_dim(slabs, 1 - c, 0, keepdims=False)
    swapped = send(yours[0], core)
    mixed = jnp.concatenate([mine[0], swapped])
    groups = [
        [flat(x, y, z, k) for z in range(Z)]
        for x in range(X)
        for y in range(Y)
        for k in range(CORES)
    ]
    rows = lax.all_gather(mixed, AXES, axis_index_groups=groups, axis=0, tiled=True)
    cols = [
        send(mine[1], rehome),
        send(yours[1], lambda x, y, z, c: rehome(x, y, z, c + 1)),
    ]
    me = me[None]
    t = own_blocks(me, offsets, amplitudes, mixed)
    t = (
        t
        + send(t, core)
        + send(t, lambda x, y, z, c: (x, y, z ^ 1, c))
        + send(t, lambda x, y, z, c: (x, y, z ^ 1, c + 1))
    )

    def near(n):
        return lambda x, y, z, c: (x + n * (1 - c), y + n * c, z, c)

    def far(n):
        return lambda x, y, z, c: (x + n * c, y + n * (1 - c), z, c)

    first = [jnp.concatenate(cols)]
    first += [send(first[0], near(n)) for n in range(1, 4)]
    t = t + sum(send(t, lambda x, y, z, c, n=n: (x, y, z ^ n, c)) for n in (2, 4, 6))
    t = t + sum(send(t, near(n)) for n in range(1, 4))
    t = jnp.pad(t, ((0, 0), (0, DEPTH - 1024)))
    cols = jnp.stack([m.reshape(8, BLK, DEPTH) for m in first])
    cols = jnp.transpose(cols, (2, 0, 1, 3)).reshape(256, DEPTH)
    second = [jnp.concatenate([cols, t])]
    second += [send(second[0], far(n)) for n in range(1, 4)]
    offdiag = (pairs[:, 0] != pairs[:, 1]).astype(jnp.float32)
    offdiag = jnp.broadcast_to(offdiag[:, None], (P_SIZE, 128))
    swap = jnp.asarray(transposed_forward(), jnp.bfloat16)
    keep, give = ladder(me, offdiag, swap, rows, second)

    taken = send(give, core)
    got = [pack(keep[0] + taken[0])]
    for k in range(1, 4):
        got.append(
            send(
                pack(keep[k] + taken[k]),
                lambda x, y, z, c, k=k: (x + k * c, y, z + 2 * k * (1 - c), c),
            )
        )

    def onward(j):
        def where(x, y, z, c):
            if c == 0:
                return x + j, y, z, c
            x, y, z, c = rehome(x, y, z, c)
            return x, y ^ (j // 2), z, c

        return where

    own = [unpack(send(piece, onward(j))) for j, piece in enumerate(route(me[0], got))]
    return finish(me, own, send(split(me, own), core))


def solution(mesh):
    in_specs = (P(), P(), P(None, "vrow", "vcol"), P(None, None, ("vrow", "vcol"), None, None))
    out_specs = P(None, "vrow", "vcol")
    return jax.shard_map(
        on_device, mesh=mesh, in_specs=in_specs, out_specs=out_specs, check_vma=False
    )
```

```python
import jax
import jax.numpy as jnp
import numpy as np
from jax import lax
from jax.experimental import pallas as pl
from jax.experimental.pallas import tpu as pltpu
from jax.sharding import PartitionSpec as P

BLK = 8
P_SIZE = 64
STEPS = 2
AXES = ("vrow", "vcol")
X, Y, Z, CORES = 4, 4, 8, 2
DEPTH = 2304
OWN = 4


SMEM = pl.BlockSpec(memory_space=pltpu.SMEM)
VMEM = pl.BlockSpec(memory_space=pltpu.VMEM)
HBM = pl.BlockSpec(memory_space=pl.ANY)


def coords(me):
    return me >> 1 & 3, me >> 4 & 3, me >> 6 << 1 | me & 1, me >> 3 & 1


def flat(x, y, z, c):
    x, y, z, c = x % X, y % Y, z % Z, c % CORES
    return z // 2 << 6 | y << 4 | c << 3 | x << 1 | z % 2


def send(block, where):
    pairs = []
    for me in range(X * Y * Z * CORES):
        pairs.append((me, flat(*where(*coords(me)))))
    return lax.ppermute(block, AXES, pairs)


def rehome(x, y, z, c):
    return x, z % 2 * 2 + y % 2, z // 2 * 2 + y // 2, c


def blocks_kernel(me, offsets, amplitudes, _, out, window, sem):
    out[...] = jnp.zeros_like(out)
    for j in range(2 * STEPS):
        first, second = offsets[j // 2, j % 2], offsets[j // 2, 1 - j % 2]
        row, at_lane = first & 31, second & 127

        @pl.when(me[0] == (first >> 5 << 3 | second >> 7))
        def _(j=j, row=row, at_lane=at_lane):
            rows = pl.ds(pl.multiple_of(row & 16, 16), 16)
            copy = pltpu.make_async_copy(amplitudes.at[:, rows, :], window, sem)
            copy.start()
            copy.wait()
            block = window[...].astype(jnp.float32)
            block = jnp.where(row & 8 == 0, block[:, :8], block[:, 8:])
            lane = lax.broadcasted_iota(jnp.int32, (P_SIZE, 128), 1)
            total = jnp.zeros((P_SIZE, 128), jnp.float32)
            for r in range(BLK):
                line = jnp.where((lane >= at_lane) & (lane < at_lane + BLK), block[:, r], 0.0)
                shift = (128 + j % 2 * 64 + r * BLK - at_lane) & 127
                total = total + pltpu.roll(line, shift, 1)
            total = total.astype(jnp.bfloat16)
            for n in range(4):
                at = 128 * (j // 2 * 4 + n)
                out[:, at : at + 128] += total[16 * n : 16 * n + 16]


def own_blocks(me, offsets, amplitudes, rows):
    return pl.pallas_call(
        blocks_kernel,
        out_shape=jax.ShapeDtypeStruct((16, 1024), jnp.bfloat16),
        in_specs=[SMEM, SMEM, HBM, HBM],
        out_specs=VMEM,
        scratch_shapes=[
            pltpu.VMEM((P_SIZE, 16, 128), jnp.bfloat16),
            pltpu.SemaphoreType.DMA(()),
        ],
        compiler_params=pltpu.CompilerParams(vmem_limit_bytes=4 << 20),
        name="blocks",
    )(me, offsets, amplitudes, rows)


def one_hot(to, dtype):
    lane = lax.broadcasted_iota(jnp.int32, (128, 128), 0)
    return jnp.where(to(lane) == lax.broadcasted_iota(jnp.int32, (128, 128), 1), 1.0, 0.0).astype(
        dtype
    )


def ladder_kernel(me, offdiag, swap, blocks, a_in, *refs):
    b_in = refs[0:4]
    keep, give = refs[4], refs[5:9]
    a_all, b_all, m_all, mine, other, sems = refs[9:]
    x, y, z, c = coords(me[0])
    copies = []
    for j in range(8):
        at = (((j // 2 - (z >> 1)) & 3) * 2 + j % 2) * 64
        copies.append(
            pltpu.make_async_copy(
                a_in.at[pl.ds(64 * j, 64), :],
                a_all.at[pl.ds(pl.multiple_of(at, 64), 64), :],
                sems.at[j],
            )
        )
    for d in range(BLK):
        for j in range(4):
            copies.append(
                pltpu.make_async_copy(
                    b_in[j].at[pl.ds(32 * d, 32), :],
                    b_all.at[d, pl.ds(32 * j, 32), :],
                    sems.at[8 + d * 4 + j],
                )
            )
    for copy in copies:
        copy.start()
    for copy in copies[:8]:
        copy.wait()
    for d in range(0, BLK, 2):
        for copy in copies[8 + 4 * d : 16 + 4 * d]:
            copy.wait()
        cols = b_all[d : d + 2].reshape(256, DEPTH)
        m = lax.dot_general(
            a_all[...], cols, (((1,), (1,)), ((), ())), preferred_element_type=jnp.float32
        )
        m_all[:, d] = m[:, :128].reshape(64, BLK, 128)
        m_all[:, d + 1] = m[:, 128:].reshape(64, BLK, 128)
    parts = []
    for n in range(4):
        one, two = (blocks[:, at : at + 128] for at in (128 * n, 128 * n + 512))
        parts.append(jnp.where(c == 0, one.astype(jnp.float32), two.astype(jnp.float32)))
    t = jnp.concatenate(parts).astype(jnp.bfloat16)
    t = jnp.dot(t, swap[...], preferred_element_type=jnp.float32)
    forward, mirror = t[:, :64], t[:, 64:]
    plus = 0.5 * (forward + mirror)
    minus = 0.5 * (forward - mirror) * offdiag[:, :64]
    u = jnp.concatenate([plus + minus, plus - minus])
    hi = u.astype(jnp.bfloat16)
    lo = (u - hi.astype(jnp.float32)).astype(jnp.bfloat16)
    left = jnp.concatenate([hi, hi, lo], axis=1)

    def target(lane):
        near, far = lane >> 3 & 3, lane >> 5
        src_x = (x - jnp.where(c == 0, near, far)) & 3
        src_y = (y - jnp.where(c == 0, far, near)) & 3
        return (
            (src_y >> 1) * 64
            + ((src_y ^ y) & 1) * 32
            + ((lane >> 2 ^ c) & 1) * 16
            + src_x * 4
            + (lane & 3)
        )

    order = one_hot(target, jnp.bfloat16)
    for g in range(32):
        w = m_all[2 * g : 2 * g + 2].reshape(128, 128)
        hi = w.astype(jnp.bfloat16)
        lo = (w - hi.astype(jnp.float32)).astype(jnp.bfloat16)
        both = jnp.dot(
            jnp.concatenate([hi, lo]), order, preferred_element_type=jnp.float32
        ).astype(jnp.bfloat16)
        parts = []
        for n in range(2):
            hi, lo = both[64 * n : 64 * n + 64], both[128 + 64 * n : 192 + 64 * n]
            parts.append(jnp.concatenate([hi, lo, hi]))
        res = jnp.dot(left, jnp.concatenate(parts, axis=1), preferred_element_type=jnp.float32)
        kz, zl, ec, i = g // 8, g // 4 % 2, g // 2 % 2, g % 2 * 2
        at = 8 * ((1 - c) if ec else c) + 4 * zl + i
        x0, x1 = res[64:, :128], res[64:, 128:]
        top = jnp.concatenate([x0[:, :64], x1[:, :64]], axis=1)
        bottom = jnp.concatenate([x0[:, 64:], x1[:, 64:]], axis=1)
        turned = jnp.concatenate([top, bottom]).T
        kx = (kz + (z >> 1) - x) & 3
        for n in range(2):
            one = res[:64, 128 * n : 128 * n + 128].reshape(4, 16, 128)
            two = turned[64 * n : 64 * n + 64].reshape(4, 16, 128)
            mine[kz, at + n] = jnp.where(c == 0, one, two)
            other[kz, at + n] = jnp.where(c == 0, two, one)
        if g % 8 == 7:
            to = keep.at[jnp.where(c == 0, kz, kx)]
            pltpu.make_async_copy(mine.at[kz], to, sems.at[kz]).start()
            for k in range(4):

                @pl.when(jnp.where(c == 0, kx, kz) == k)
                def _(kz=kz, k=k):
                    pltpu.make_async_copy(other.at[kz], give[k], sems.at[4 + kz]).start()

    for kz in range(4):
        pltpu.make_async_copy(mine.at[kz], keep.at[kz], sems.at[kz]).wait()
        pltpu.make_async_copy(other.at[kz], give[kz], sems.at[4 + kz]).wait()


def ladder(me, offdiag, swap, blocks, rows, cols):
    f32, bf16 = jnp.float32, jnp.bfloat16
    return pl.pallas_call(
        ladder_kernel,
        out_shape=[jax.ShapeDtypeStruct((4, 16, 4, 16, 128), f32)]
        + [jax.ShapeDtypeStruct((16, 4, 16, 128), f32)] * 4,
        in_specs=[SMEM, VMEM, VMEM, VMEM] + [HBM] * 5,
        out_specs=[HBM] * 5,
        scratch_shapes=[
            pltpu.VMEM((512, DEPTH), bf16),
            pltpu.VMEM((BLK, 128, DEPTH), bf16),
            pltpu.VMEM((64, BLK, BLK, 128), f32),
            pltpu.VMEM((4, 16, 4, 16, 128), f32),
            pltpu.VMEM((4, 16, 4, 16, 128), f32),
            pltpu.SemaphoreType.DMA((40,)),
        ],
        compiler_params=pltpu.CompilerParams(vmem_limit_bytes=56 << 20),
        name="ladder",
    )(me, offdiag, swap, blocks, rows, *cols)


def pack(block):
    top = jnp.max(jnp.abs(block), axis=0, keepdims=True)
    power = jnp.clip(jnp.floor(jnp.log2(top)), -100.0, 100.0)
    return jnp.concatenate([block * jnp.exp2(14.0 - power), power]).astype(jnp.float16)


def unpack(block):
    block = block.astype(jnp.float32)
    return block[:16] * jnp.exp2(block[16:] - 14.0)


def route(me, got):
    x, _, z, c = coords(me)
    every = jnp.stack(got)
    out = []
    for j in range(4):
        whole = lax.dynamic_index_in_dim(every, ((z >> 1) - x - j) & 3, 0, keepdims=False)
        e, k = j // 2, j % 2 * 2
        rows = [got[k + n][:, 2 * e : 2 * e + 2] for n in range(2)]
        out.append(jnp.where(c == 0, whole, jnp.concatenate(rows, axis=1)))
    return out


def split_kernel(me, *refs):
    own, out = refs[:4], refs[4]
    c = coords(me[0])[3]

    @pl.when(c == 0)
    def _():
        for j in range(4):
            out[j] = own[j][8:]

    @pl.when(c == 1)
    def _():
        for j in range(4):
            for a5 in range(2):
                for k in range(2):
                    out[j, :, 2 * a5 + k] = own[j][8 * a5 : 8 * a5 + 8, 2 * k]


def split(me, own):
    return pl.pallas_call(
        split_kernel,
        out_shape=jax.ShapeDtypeStruct((4, 8, 4, 16, 128), own[0].dtype),
        in_specs=[SMEM] + [VMEM] * 4,
        out_specs=VMEM,
        compiler_params=pltpu.CompilerParams(vmem_limit_bytes=10 << 20),
        name="split",
    )(me, *own)


def finish_kernel(me, *refs):
    own, other, out = refs[:4], refs[4], refs[5]
    r1, r2 = refs[6:]
    x, y, _, c = coords(me[0])

    def fetch(core):
        for j in range(4):
            r1[(x - j) & 3] = other[j] if core else own[j][:8]
            for a5 in range(2):
                for k in range(2):
                    if core:
                        block = own[j][8 * a5 : 8 * a5 + 8, 2 * k + 1]
                    else:
                        block = other[j, :, 2 * a5 + k]
                    r2[(y & 1) ^ (j // 2), a5, (x - 2 * (j % 2) - k) & 3] = block

    for core in range(2):

        @pl.when(c == core)
        def _(core=core):
            fetch(core)

    order = one_hot(
        lambda lane: ((lane >> 5 ^ y) & 1) * 64
        + (lane >> 4 & 1) * 32
        + (lane >> 2 & 3) * 8
        + (lane >> 6) * 4
        + (lane & 3),
        jnp.bfloat16,
    )
    for g in range(4):
        t = r1[g].reshape(8 * P_SIZE, 128)
        hi = t.astype(jnp.bfloat16)
        lo = (t - hi.astype(jnp.float32)).astype(jnp.bfloat16)
        t = jnp.dot(hi, order, preferred_element_type=jnp.float32) + jnp.dot(
            lo, order, preferred_element_type=jnp.float32
        )
        for n in range(8):
            out[:, 8 * g + n, :] = t[64 * n : 64 * n + 64]
    for r in range(16):
        t = r2[:, :, :, :, r, :].reshape(128, 128).T
        for b2 in range(2):
            row = r // 4 * 8 + b2 * 4 + r % 4
            out[:, row, :] = out[:, row, :] + t[64 * b2 : 64 * b2 + 64]


def finish(me, own, other):
    f32 = jnp.float32
    return pl.pallas_call(
        finish_kernel,
        out_shape=jax.ShapeDtypeStruct((P_SIZE, 32, 128), f32),
        in_specs=[SMEM] + [VMEM] * 5,
        out_specs=VMEM,
        scratch_shapes=[
            pltpu.VMEM((4, 8, 4, 16, 128), f32),
            pltpu.VMEM((2, 2, 4, 8, 16, 128), f32),
        ],
        compiler_params=pltpu.CompilerParams(vmem_limit_bytes=16 << 20),
        name="finish",
    )(me, *own, other)


def transposed_forward():
    m = np.zeros((128, 128), np.float32)
    for c in range(BLK):
        for d in range(BLK):
            m[c * BLK + d, d * BLK + c] = 1
            m[64 + d * BLK + c, 64 + d * BLK + c] = 1
    return m


def on_device(pairs, offsets, amplitudes, slabs):
    me = lax.axis_index(AXES)
    c = me >> 3 & 1
    core = lambda x, y, z, c: (x, y, z, c + 1)
    slabs = slabs.reshape(STEPS, 2, OWN * BLK, DEPTH)
    mine = lax.dynamic_index_in_dim(slabs, c, 0, keepdims=False)
    yours = lax.dynamic_index_in_dim(slabs, 1 - c, 0, keepdims=False)
    swapped = send(yours[0], core)
    mixed = jnp.concatenate([mine[0], swapped])
    groups = [
        [flat(x, y, z, k) for z in range(Z)]
        for x in range(X)
        for y in range(Y)
        for k in range(CORES)
    ]
    rows = lax.all_gather(mixed, AXES, axis_index_groups=groups, axis=0, tiled=True)
    cols = [
        send(mine[1], rehome),
        send(yours[1], lambda x, y, z, c: rehome(x, y, z, c + 1)),
    ]
    me = me[None]
    t = own_blocks(me, offsets, amplitudes, mixed)
    t = (
        t
        + send(t, core)
        + send(t, lambda x, y, z, c: (x, y, z ^ 1, c))
        + send(t, lambda x, y, z, c: (x, y, z ^ 1, c + 1))
    )

    def near(n):
        return lambda x, y, z, c: (x + n * (1 - c), y + n * c, z, c)

    def far(n):
        return lambda x, y, z, c: (x + n * c, y + n * (1 - c), z, c)

    t = jnp.pad(t, ((0, 0), (0, DEPTH - 1024)))
    first = [jnp.concatenate(cols + [t])]
    first += [send(first[0], near(n)) for n in range(1, 4)]
    cols = jnp.stack([m[:64].reshape(8, BLK, DEPTH) for m in first])
    cols = jnp.transpose(cols, (2, 0, 1, 3)).reshape(256, DEPTH)
    second = [cols] + [send(cols, far(n)) for n in range(1, 4)]
    t = sum(m[64:, :1024] for m in first[1:]) + first[0][64:, :1024]
    t = t + cols[:16, :1024] * 0
    t = t + sum(send(t, lambda x, y, z, c, n=n: (x, y, z ^ n, c)) for n in (2, 4, 6))
    t = t + sum(send(t, far(n)) for n in range(1, 4))
    offdiag = (pairs[:, 0] != pairs[:, 1]).astype(jnp.float32)
    offdiag = jnp.broadcast_to(offdiag[:, None], (P_SIZE, 128))
    swap = jnp.asarray(transposed_forward(), jnp.bfloat16)
    keep, *give = ladder(me, offdiag, swap, t, rows, second)

    got = [pack(keep[k] + send(give[k], core)) for k in range(4)]
    for k in range(1, 4):
        got[k] = send(got[k], lambda x, y, z, c, k=k: (x + k * c, y, z + 2 * k * (1 - c), c))

    def onward(j):
        def where(x, y, z, c):
            if c == 0:
                return x + j, y, z, c
            x, y, z, c = rehome(x, y, z, c)
            return x, y ^ (j // 2), z, c

        return where

    own = [unpack(send(piece, onward(j))) for j, piece in enumerate(route(me[0], got))]
    return finish(me, own, send(split(me, own), core))


def solution(mesh):
    in_specs = (P(), P(), P(None, "vrow", "vcol"), P(None, None, ("vrow", "vcol"), None, None))
    out_specs = P(None, "vrow", "vcol")
    return jax.shard_map(
        on_device, mesh=mesh, in_specs=in_specs, out_specs=out_specs, check_vma=False
    )
```

```python
import jax
import jax.numpy as jnp
import numpy as np
from jax import lax
from jax.experimental import pallas as pl
from jax.experimental.pallas import tpu as pltpu
from jax.sharding import PartitionSpec as P

BLK = 8
P_SIZE = 64
STEPS = 2
AXES = ("vrow", "vcol")
X, Y, Z, CORES = 4, 4, 8, 2
DEPTH = 2304
OWN = 4


SMEM = pl.BlockSpec(memory_space=pltpu.SMEM)
VMEM = pl.BlockSpec(memory_space=pltpu.VMEM)
HBM = pl.BlockSpec(memory_space=pl.ANY)


def coords(me):
    return me >> 1 & 3, me >> 4 & 3, me >> 6 << 1 | me & 1, me >> 3 & 1


def flat(x, y, z, c):
    x, y, z, c = x % X, y % Y, z % Z, c % CORES
    return z // 2 << 6 | y << 4 | c << 3 | x << 1 | z % 2


def send(block, where):
    pairs = []
    for me in range(X * Y * Z * CORES):
        pairs.append((me, flat(*where(*coords(me)))))
    return lax.ppermute(block, AXES, pairs)


def rehome(x, y, z, c):
    return x, z % 2 * 2 + y % 2, z // 2 * 2 + y // 2, c


def blocks_kernel(me, offsets, amplitudes, _, out, window, sem):
    out[...] = jnp.zeros_like(out)
    for j in range(2 * STEPS):
        first, second = offsets[j // 2, j % 2], offsets[j // 2, 1 - j % 2]
        row, at_lane = first & 31, second & 127

        @pl.when(me[0] == (first >> 5 << 3 | second >> 7))
        def _(j=j, row=row, at_lane=at_lane):
            rows = pl.ds(pl.multiple_of(row & 16, 16), 16)
            copy = pltpu.make_async_copy(amplitudes.at[:, rows, :], window, sem)
            copy.start()
            copy.wait()
            block = window[...].astype(jnp.float32)
            block = jnp.where(row & 8 == 0, block[:, :8], block[:, 8:])
            lane = lax.broadcasted_iota(jnp.int32, (P_SIZE, 128), 1)
            total = jnp.zeros((P_SIZE, 128), jnp.float32)
            for r in range(BLK):
                line = jnp.where((lane >= at_lane) & (lane < at_lane + BLK), block[:, r], 0.0)
                shift = (128 + j % 2 * 64 + r * BLK - at_lane) & 127
                total = total + pltpu.roll(line, shift, 1)
            total = total.astype(jnp.bfloat16)
            for n in range(4):
                at = 128 * (j // 2 * 4 + n)
                out[:, at : at + 128] += total[16 * n : 16 * n + 16]


def own_blocks(me, offsets, amplitudes, rows):
    return pl.pallas_call(
        blocks_kernel,
        out_shape=jax.ShapeDtypeStruct((16, 1024), jnp.bfloat16),
        in_specs=[SMEM, SMEM, HBM, HBM],
        out_specs=VMEM,
        scratch_shapes=[
            pltpu.VMEM((P_SIZE, 16, 128), jnp.bfloat16),
            pltpu.SemaphoreType.DMA(()),
        ],
        compiler_params=pltpu.CompilerParams(vmem_limit_bytes=4 << 20),
        name="blocks",
    )(me, offsets, amplitudes, rows)


def one_hot(to, dtype):
    lane = lax.broadcasted_iota(jnp.int32, (128, 128), 0)
    return jnp.where(to(lane) == lax.broadcasted_iota(jnp.int32, (128, 128), 1), 1.0, 0.0).astype(
        dtype
    )


def ladder_kernel(me, offdiag, swap, blocks, a_in, *refs):
    b_in = refs[0:4]
    keep, give = refs[4], refs[5:9]
    a_all, b_all, m_all, mine, other, sems = refs[9:]
    x, y, z, c = coords(me[0])
    copies = []
    for j in range(8):
        at = (((j // 2 - (z >> 1)) & 3) * 2 + j % 2) * 64
        copies.append(
            pltpu.make_async_copy(
                a_in.at[pl.ds(64 * j, 64), :],
                a_all.at[pl.ds(pl.multiple_of(at, 64), 64), :],
                sems.at[j],
            )
        )
    for d in range(BLK):
        for j in range(4):
            copies.append(
                pltpu.make_async_copy(
                    b_in[j].at[pl.ds(32 * d, 32), :],
                    b_all.at[d, pl.ds(32 * j, 32), :],
                    sems.at[8 + d * 4 + j],
                )
            )
    for copy in copies:
        copy.start()
    for copy in copies[:8]:
        copy.wait()
    for d in range(0, BLK, 2):
        for copy in copies[8 + 4 * d : 16 + 4 * d]:
            copy.wait()
        cols = b_all[d : d + 2].reshape(256, DEPTH)
        m = lax.dot_general(
            a_all[...], cols, (((1,), (1,)), ((), ())), preferred_element_type=jnp.float32
        )
        m_all[:, d] = m[:, :128].reshape(64, BLK, 128)
        m_all[:, d + 1] = m[:, 128:].reshape(64, BLK, 128)
    parts = []
    for n in range(4):
        one, two = (blocks[:, at : at + 128] for at in (128 * n, 128 * n + 512))
        parts.append(jnp.where(c == 0, one.astype(jnp.float32), two.astype(jnp.float32)))
    t = jnp.concatenate(parts).astype(jnp.bfloat16)
    t = jnp.dot(t, swap[...], preferred_element_type=jnp.float32)
    forward, mirror = t[:, :64], t[:, 64:]
    plus = 0.5 * (forward + mirror)
    minus = 0.5 * (forward - mirror) * offdiag[:, :64]
    u = jnp.concatenate([plus + minus, plus - minus])
    hi = u.astype(jnp.bfloat16)
    lo = (u - hi.astype(jnp.float32)).astype(jnp.bfloat16)
    left = jnp.concatenate([hi, hi, lo], axis=1)

    def target(lane):
        near, far = lane >> 3 & 3, lane >> 5
        src_x = (x - jnp.where(c == 0, near, far)) & 3
        src_y = (y - jnp.where(c == 0, far, near)) & 3
        return (
            (src_y >> 1) * 64
            + ((src_y ^ y) & 1) * 32
            + ((lane >> 2 ^ c) & 1) * 16
            + src_x * 4
            + (lane & 3)
        )

    order = one_hot(target, jnp.bfloat16)
    for g in range(32):
        w = m_all[2 * g : 2 * g + 2].reshape(128, 128)
        hi = w.astype(jnp.bfloat16)
        lo = (w - hi.astype(jnp.float32)).astype(jnp.bfloat16)
        both = jnp.dot(
            jnp.concatenate([hi, lo]), order, preferred_element_type=jnp.float32
        ).astype(jnp.bfloat16)
        parts = []
        for n in range(2):
            hi, lo = both[64 * n : 64 * n + 64], both[128 + 64 * n : 192 + 64 * n]
            parts.append(jnp.concatenate([hi, lo, hi]))
        res = jnp.dot(left, jnp.concatenate(parts, axis=1), preferred_element_type=jnp.float32)
        kz, zl, ec, i = g // 8, g // 4 % 2, g // 2 % 2, g % 2 * 2
        at = 8 * ((1 - c) if ec else c) + 4 * zl + i
        x0, x1 = res[64:, :128], res[64:, 128:]
        top = jnp.concatenate([x0[:, :64], x1[:, :64]], axis=1)
        bottom = jnp.concatenate([x0[:, 64:], x1[:, 64:]], axis=1)
        turned = jnp.concatenate([top, bottom]).T
        kx = (kz + (z >> 1) - x) & 3
        for n in range(2):
            one = res[:64, 128 * n : 128 * n + 128].reshape(4, 16, 128)
            two = turned[64 * n : 64 * n + 64].reshape(4, 16, 128)
            mine[kz, at + n] = jnp.where(c == 0, one, two)
            other[kz, at + n] = jnp.where(c == 0, two, one)
        if g % 8 == 7:
            mine[kz, 16] = jnp.max(jnp.abs(mine[kz, :16]), axis=0)
            other[kz, 16] = jnp.max(jnp.abs(other[kz, :16]), axis=0)
            to = keep.at[jnp.where(c == 0, kz, kx)]
            pltpu.make_async_copy(mine.at[kz], to, sems.at[kz]).start()
            for k in range(4):

                @pl.when(jnp.where(c == 0, kx, kz) == k)
                def _(kz=kz, k=k):
                    pltpu.make_async_copy(other.at[kz], give[k], sems.at[4 + kz]).start()

    for kz in range(4):
        pltpu.make_async_copy(mine.at[kz], keep.at[kz], sems.at[kz]).wait()
        pltpu.make_async_copy(other.at[kz], give[kz], sems.at[4 + kz]).wait()


def ladder(me, offdiag, swap, blocks, rows, cols):
    f32, bf16 = jnp.float32, jnp.bfloat16
    return pl.pallas_call(
        ladder_kernel,
        out_shape=[jax.ShapeDtypeStruct((4, 17, 4, 16, 128), f32)]
        + [jax.ShapeDtypeStruct((17, 4, 16, 128), f32)] * 4,
        in_specs=[SMEM, VMEM, VMEM, VMEM] + [HBM] * 5,
        out_specs=[HBM] * 5,
        scratch_shapes=[
            pltpu.VMEM((512, DEPTH), bf16),
            pltpu.VMEM((BLK, 128, DEPTH), bf16),
            pltpu.VMEM((64, BLK, BLK, 128), f32),
            pltpu.VMEM((4, 17, 4, 16, 128), f32),
            pltpu.VMEM((4, 17, 4, 16, 128), f32),
            pltpu.SemaphoreType.DMA((40,)),
        ],
        compiler_params=pltpu.CompilerParams(vmem_limit_bytes=56 << 20),
        name="ladder",
    )(me, offdiag, swap, blocks, rows, *cols)


def pack(block):
    power = jnp.clip(jnp.floor(jnp.log2(block[16:])), -100.0, 100.0)
    return jnp.concatenate([block[:16] * jnp.exp2(14.0 - power), power]).astype(jnp.float16)


def unpack(block):
    block = block.astype(jnp.float32)
    return block[:16] * jnp.exp2(block[16:] - 14.0)


def route(me, got):
    x, _, z, c = coords(me)
    every = jnp.stack(got)
    out = []
    for j in range(4):
        whole = lax.dynamic_index_in_dim(every, ((z >> 1) - x - j) & 3, 0, keepdims=False)
        e, k = j // 2, j % 2 * 2
        rows = [got[k + n][:, 2 * e : 2 * e + 2] for n in range(2)]
        out.append(jnp.where(c == 0, whole, jnp.concatenate(rows, axis=1)))
    return out


def split_kernel(me, *refs):
    own, out = refs[:4], refs[4]
    c = coords(me[0])[3]

    @pl.when(c == 0)
    def _():
        for j in range(4):
            out[j] = own[j][8:]

    @pl.when(c == 1)
    def _():
        for j in range(4):
            for a5 in range(2):
                for k in range(2):
                    out[j, :, 2 * a5 + k] = own[j][8 * a5 : 8 * a5 + 8, 2 * k]


def split(me, own):
    return pl.pallas_call(
        split_kernel,
        out_shape=jax.ShapeDtypeStruct((4, 8, 4, 16, 128), own[0].dtype),
        in_specs=[SMEM] + [VMEM] * 4,
        out_specs=VMEM,
        compiler_params=pltpu.CompilerParams(vmem_limit_bytes=10 << 20),
        name="split",
    )(me, *own)


def finish_kernel(me, *refs):
    own, other, out = refs[:4], refs[4], refs[5]
    r1, r2 = refs[6:]
    x, y, _, c = coords(me[0])

    def fetch(core):
        for j in range(4):
            r1[(x - j) & 3] = other[j] if core else own[j][:8]
            for a5 in range(2):
                for k in range(2):
                    if core:
                        block = own[j][8 * a5 : 8 * a5 + 8, 2 * k + 1]
                    else:
                        block = other[j, :, 2 * a5 + k]
                    r2[(y & 1) ^ (j // 2), a5, (x - 2 * (j % 2) - k) & 3] = block

    for core in range(2):

        @pl.when(c == core)
        def _(core=core):
            fetch(core)

    order = one_hot(
        lambda lane: ((lane >> 5 ^ y) & 1) * 64
        + (lane >> 4 & 1) * 32
        + (lane >> 2 & 3) * 8
        + (lane >> 6) * 4
        + (lane & 3),
        jnp.bfloat16,
    )
    for g in range(4):
        t = r1[g].reshape(8 * P_SIZE, 128)
        hi = t.astype(jnp.bfloat16)
        lo = (t - hi.astype(jnp.float32)).astype(jnp.bfloat16)
        t = jnp.dot(hi, order, preferred_element_type=jnp.float32) + jnp.dot(
            lo, order, preferred_element_type=jnp.float32
        )
        r1[g] = t.reshape(8, 4, 16, 128)
    for r in range(16):
        t = r2[:, :, :, :, r, :].reshape(128, 128).T
        for b2 in range(2):
            row = r // 4 * 8 + b2 * 4 + r % 4
            one = r1[row // 8, row % 8].reshape(P_SIZE, 128)
            out[:, row, :] = one + t[64 * b2 : 64 * b2 + 64]


def finish(me, own, other):
    f32 = jnp.float32
    return pl.pallas_call(
        finish_kernel,
        out_shape=jax.ShapeDtypeStruct((P_SIZE, 32, 128), f32),
        in_specs=[SMEM] + [VMEM] * 5,
        out_specs=VMEM,
        scratch_shapes=[
            pltpu.VMEM((4, 8, 4, 16, 128), f32),
            pltpu.VMEM((2, 2, 4, 8, 16, 128), f32),
        ],
        compiler_params=pltpu.CompilerParams(vmem_limit_bytes=16 << 20),
        name="finish",
    )(me, *own, other)


def transposed_forward():
    m = np.zeros((128, 128), np.float32)
    for c in range(BLK):
        for d in range(BLK):
            m[c * BLK + d, d * BLK + c] = 1
            m[64 + d * BLK + c, 64 + d * BLK + c] = 1
    return m


def on_device(pairs, offsets, amplitudes, slabs):
    me = lax.axis_index(AXES)
    c = me >> 3 & 1
    core = lambda x, y, z, c: (x, y, z, c + 1)
    slabs = slabs.reshape(STEPS, 2, OWN * BLK, DEPTH)
    mine = lax.dynamic_index_in_dim(slabs, c, 0, keepdims=False)
    yours = lax.dynamic_index_in_dim(slabs, 1 - c, 0, keepdims=False)
    swapped = send(yours[0], core)
    mixed = jnp.concatenate([mine[0], swapped])
    groups = [
        [flat(x, y, z, k) for z in range(Z)]
        for x in range(X)
        for y in range(Y)
        for k in range(CORES)
    ]
    rows = lax.all_gather(mixed, AXES, axis_index_groups=groups, axis=0, tiled=True)
    cols = [
        send(mine[1], rehome),
        send(yours[1], lambda x, y, z, c: rehome(x, y, z, c + 1)),
    ]
    me = me[None]
    t = own_blocks(me, offsets, amplitudes, mixed)
    t = (
        t
        + send(t, core)
        + send(t, lambda x, y, z, c: (x, y, z ^ 1, c))
        + send(t, lambda x, y, z, c: (x, y, z ^ 1, c + 1))
    )

    def near(n):
        return lambda x, y, z, c: (x + n * (1 - c), y + n * c, z, c)

    def far(n):
        return lambda x, y, z, c: (x + n * c, y + n * (1 - c), z, c)

    t = jnp.pad(t, ((0, 0), (0, DEPTH - 1024)))
    first = [jnp.concatenate(cols + [t])]
    first += [send(first[0], near(n)) for n in range(1, 4)]
    cols = jnp.stack([m[:64].reshape(8, BLK, DEPTH) for m in first])
    cols = jnp.transpose(cols, (2, 0, 1, 3)).reshape(256, DEPTH)
    second = [cols] + [send(cols, far(n)) for n in range(1, 4)]
    t = sum(m[64:, :1024] for m in first[1:]) + first[0][64:, :1024]
    t = t + cols[:16, :1024] * 0
    t = t + sum(send(t, lambda x, y, z, c, n=n: (x, y, z ^ n, c)) for n in (2, 4, 6))
    t = t + sum(send(t, far(n)) for n in range(1, 4))
    offdiag = (pairs[:, 0] != pairs[:, 1]).astype(jnp.float32)
    offdiag = jnp.broadcast_to(offdiag[:, None], (P_SIZE, 128))
    swap = jnp.asarray(transposed_forward(), jnp.bfloat16)
    keep, *give = ladder(me, offdiag, swap, t, rows, second)

    got = [pack(keep[k] + send(give[k], core)) for k in range(4)]
    for k in range(1, 4):
        got[k] = send(got[k], lambda x, y, z, c, k=k: (x + k * c, y, z + 2 * k * (1 - c), c))

    def onward(j):
        def where(x, y, z, c):
            if c == 0:
                return x + j, y, z, c
            x, y, z, c = rehome(x, y, z, c)
            return x, y ^ (j // 2), z, c

        return where

    own = [unpack(send(piece, onward(j))) for j, piece in enumerate(route(me[0], got))]
    return finish(me, own, send(split(me, own), core))


def solution(mesh):
    in_specs = (P(), P(), P(None, "vrow", "vcol"), P(None, None, ("vrow", "vcol"), None, None))
    out_specs = P(None, "vrow", "vcol")
    return jax.shard_map(
        on_device, mesh=mesh, in_specs=in_specs, out_specs=out_specs, check_vma=False
    )
```

```python
import jax
import jax.numpy as jnp
import numpy as np
from jax import lax
from jax.experimental import pallas as pl
from jax.experimental.pallas import tpu as pltpu
from jax.sharding import PartitionSpec as P

BLK = 8
P_SIZE = 64
STEPS = 2
AXES = ("vrow", "vcol")
X, Y, Z, CORES = 4, 4, 8, 2
DEPTH = 2304
OWN = 4


SMEM = pl.BlockSpec(memory_space=pltpu.SMEM)
VMEM = pl.BlockSpec(memory_space=pltpu.VMEM)
HBM = pl.BlockSpec(memory_space=pl.ANY)


def coords(me):
    return me >> 1 & 3, me >> 4 & 3, me >> 6 << 1 | me & 1, me >> 3 & 1


def flat(x, y, z, c):
    x, y, z, c = x % X, y % Y, z % Z, c % CORES
    return z // 2 << 6 | y << 4 | c << 3 | x << 1 | z % 2


def send(block, where):
    pairs = []
    for me in range(X * Y * Z * CORES):
        pairs.append((me, flat(*where(*coords(me)))))
    return lax.ppermute(block, AXES, pairs)


def rehome(x, y, z, c):
    return x, z % 2 * 2 + y % 2, z // 2 * 2 + y // 2, c


def blocks_kernel(me, offsets, amplitudes, _, out, window, sem):
    out[...] = jnp.zeros_like(out)
    for j in range(2 * STEPS):
        first, second = offsets[j // 2, j % 2], offsets[j // 2, 1 - j % 2]
        row, at_lane = first & 31, second & 127

        @pl.when(me[0] == (first >> 5 << 3 | second >> 7))
        def _(j=j, row=row, at_lane=at_lane):
            rows = pl.ds(pl.multiple_of(row & 16, 16), 16)
            copy = pltpu.make_async_copy(amplitudes.at[:, rows, :], window, sem)
            copy.start()
            copy.wait()
            block = window[...].astype(jnp.float32)
            block = jnp.where(row & 8 == 0, block[:, :8], block[:, 8:])
            lane = lax.broadcasted_iota(jnp.int32, (P_SIZE, 128), 1)
            total = jnp.zeros((P_SIZE, 128), jnp.float32)
            for r in range(BLK):
                line = jnp.where((lane >= at_lane) & (lane < at_lane + BLK), block[:, r], 0.0)
                shift = (128 + j % 2 * 64 + r * BLK - at_lane) & 127
                total = total + pltpu.roll(line, shift, 1)
            total = total.astype(jnp.bfloat16)
            for n in range(4):
                at = 128 * (j // 2 * 4 + n)
                out[:, at : at + 128] += total[16 * n : 16 * n + 16]


def own_blocks(me, offsets, amplitudes, rows):
    return pl.pallas_call(
        blocks_kernel,
        out_shape=jax.ShapeDtypeStruct((16, 1024), jnp.bfloat16),
        in_specs=[SMEM, SMEM, HBM, HBM],
        out_specs=VMEM,
        scratch_shapes=[
            pltpu.VMEM((P_SIZE, 16, 128), jnp.bfloat16),
            pltpu.SemaphoreType.DMA(()),
        ],
        compiler_params=pltpu.CompilerParams(vmem_limit_bytes=4 << 20),
        name="blocks",
    )(me, offsets, amplitudes, rows)


def one_hot(to, dtype):
    lane = lax.broadcasted_iota(jnp.int32, (128, 128), 0)
    return jnp.where(to(lane) == lax.broadcasted_iota(jnp.int32, (128, 128), 1), 1.0, 0.0).astype(
        dtype
    )


def ladder_kernel(me, offdiag, swap, blocks, a_in, *refs):
    b_in = refs[0:4]
    keep, give = refs[4], refs[5:9]
    a_all, b_all, m_all, mine, other, sems = refs[9:]
    x, y, z, c = coords(me[0])
    copies = []
    for j in range(8):
        at = (((j // 2 - (z >> 1)) & 3) * 2 + j % 2) * 64
        copies.append(
            pltpu.make_async_copy(
                a_in.at[pl.ds(64 * j, 64), :],
                a_all.at[pl.ds(pl.multiple_of(at, 64), 64), :],
                sems.at[j],
            )
        )
    for d in range(BLK):
        for j in range(4):
            copies.append(
                pltpu.make_async_copy(
                    b_in[j].at[pl.ds(32 * d, 32), :],
                    b_all.at[d, pl.ds(32 * j, 32), :],
                    sems.at[8 + d * 4 + j],
                )
            )
    for copy in copies:
        copy.start()
    for copy in copies[:8]:
        copy.wait()
    for d in range(0, BLK, 2):
        for copy in copies[8 + 4 * d : 16 + 4 * d]:
            copy.wait()
        cols = b_all[d : d + 2].reshape(256, DEPTH)
        m = lax.dot_general(
            a_all[...], cols, (((1,), (1,)), ((), ())), preferred_element_type=jnp.float32
        )
        m_all[:, d] = m[:, :128].reshape(64, BLK, 128)
        m_all[:, d + 1] = m[:, 128:].reshape(64, BLK, 128)
    parts = []
    for n in range(4):
        one, two = (blocks[:, at : at + 128] for at in (128 * n, 128 * n + 512))
        parts.append(jnp.where(c == 0, one.astype(jnp.float32), two.astype(jnp.float32)))
    t = jnp.concatenate(parts).astype(jnp.bfloat16)
    t = jnp.dot(t, swap[...], preferred_element_type=jnp.float32)
    forward, mirror = t[:, :64], t[:, 64:]
    plus = 0.5 * (forward + mirror)
    minus = 0.5 * (forward - mirror) * offdiag[:, :64]
    u = jnp.concatenate([plus + minus, plus - minus])
    hi = u.astype(jnp.bfloat16)
    lo = (u - hi.astype(jnp.float32)).astype(jnp.bfloat16)
    left = jnp.concatenate([hi, hi, lo], axis=1)

    def target(lane):
        near, far = lane >> 3 & 3, lane >> 5
        src_x = (x - jnp.where(c == 0, near, far)) & 3
        src_y = (y - jnp.where(c == 0, far, near)) & 3
        return (
            (src_y >> 1) * 64
            + ((src_y ^ y) & 1) * 32
            + ((lane >> 2 ^ c) & 1) * 16
            + src_x * 4
            + (lane & 3)
        )

    order = one_hot(target, jnp.bfloat16)
    for g in range(32):
        w = m_all[2 * g : 2 * g + 2].reshape(128, 128)
        hi = w.astype(jnp.bfloat16)
        lo = (w - hi.astype(jnp.float32)).astype(jnp.bfloat16)
        both = jnp.dot(
            jnp.concatenate([hi, lo]), order, preferred_element_type=jnp.float32
        ).astype(jnp.bfloat16)
        parts = []
        for n in range(2):
            hi, lo = both[64 * n : 64 * n + 64], both[128 + 64 * n : 192 + 64 * n]
            parts.append(jnp.concatenate([hi, lo, hi]))
        res = jnp.dot(left, jnp.concatenate(parts, axis=1), preferred_element_type=jnp.float32)
        kz, zl, ec, i = g // 8, g // 4 % 2, g // 2 % 2, g % 2 * 2
        at = 8 * ((1 - c) if ec else c) + 4 * zl + i
        x0, x1 = res[64:, :128], res[64:, 128:]
        top = jnp.concatenate([x0[:, :64], x1[:, :64]], axis=1)
        bottom = jnp.concatenate([x0[:, 64:], x1[:, 64:]], axis=1)
        turned = jnp.concatenate([top, bottom]).T
        kx = (kz + (z >> 1) - x) & 3
        for n in range(2):
            one = res[:64, 128 * n : 128 * n + 128].reshape(4, 16, 128)
            two = turned[64 * n : 64 * n + 64].reshape(4, 16, 128)
            mine[kz, at + n] = jnp.where(c == 0, one, two)
            other[kz, at + n] = jnp.where(c == 0, two, one)
        if g % 8 == 7:
            mine[kz, 16] = jnp.max(jnp.abs(mine[kz, :16]), axis=0)
            other[kz, 16] = jnp.max(jnp.abs(other[kz, :16]), axis=0)
            to = keep.at[jnp.where(c == 0, kz, kx)]
            pltpu.make_async_copy(mine.at[kz], to, sems.at[kz]).start()
            for k in range(4):

                @pl.when(jnp.where(c == 0, kx, kz) == k)
                def _(kz=kz, k=k):
                    pltpu.make_async_copy(other.at[kz], give[k], sems.at[4 + kz]).start()

    for kz in range(4):
        pltpu.make_async_copy(mine.at[kz], keep.at[kz], sems.at[kz]).wait()
        pltpu.make_async_copy(other.at[kz], give[kz], sems.at[4 + kz]).wait()


def ladder(me, offdiag, swap, blocks, rows, cols):
    f32, bf16 = jnp.float32, jnp.bfloat16
    return pl.pallas_call(
        ladder_kernel,
        out_shape=[jax.ShapeDtypeStruct((4, 17, 4, 16, 128), f32)]
        + [jax.ShapeDtypeStruct((17, 4, 16, 128), f32)] * 4,
        in_specs=[SMEM, VMEM, VMEM, VMEM] + [HBM] * 5,
        out_specs=[HBM] * 5,
        scratch_shapes=[
            pltpu.VMEM((512, DEPTH), bf16),
            pltpu.VMEM((BLK, 128, DEPTH), bf16),
            pltpu.VMEM((64, BLK, BLK, 128), f32),
            pltpu.VMEM((4, 17, 4, 16, 128), f32),
            pltpu.VMEM((4, 17, 4, 16, 128), f32),
            pltpu.SemaphoreType.DMA((40,)),
        ],
        compiler_params=pltpu.CompilerParams(vmem_limit_bytes=56 << 20),
        name="ladder",
    )(me, offdiag, swap, blocks, rows, *cols)


def pack(block):
    power = jnp.clip(jnp.floor(jnp.log2(block[16:])), -100.0, 100.0)
    return jnp.concatenate([block[:16] * jnp.exp2(14.0 - power), power]).astype(jnp.float16)


def unpack(block):
    block = block.astype(jnp.float32)
    return block[:16] * jnp.exp2(block[16:] - 14.0)


def route(me, got):
    x, _, z, c = coords(me)
    every = jnp.stack(got)
    out = []
    for j in range(4):
        whole = lax.dynamic_index_in_dim(every, ((z >> 1) - x - j) & 3, 0, keepdims=False)
        e, k = j // 2, j % 2 * 2
        rows = [got[k + n][:, 2 * e : 2 * e + 2] for n in range(2)]
        out.append(jnp.where(c == 0, whole, jnp.concatenate(rows, axis=1)))
    return out


def split_kernel(me, *refs):
    own, out = refs[:4], refs[4]
    c = coords(me[0])[3]

    @pl.when(c == 0)
    def _():
        for j in range(4):
            out[j] = own[j][8:]

    @pl.when(c == 1)
    def _():
        for j in range(4):
            for a5 in range(2):
                for k in range(2):
                    out[j, :, 2 * a5 + k] = own[j][8 * a5 : 8 * a5 + 8, 2 * k]


def split(me, own):
    return pl.pallas_call(
        split_kernel,
        out_shape=jax.ShapeDtypeStruct((4, 8, 4, 16, 128), own[0].dtype),
        in_specs=[SMEM] + [VMEM] * 4,
        out_specs=VMEM,
        compiler_params=pltpu.CompilerParams(vmem_limit_bytes=10 << 20),
        name="split",
    )(me, *own)


def finish_kernel(me, *refs):
    own, other, out = refs[:4], refs[4], refs[5]
    r1, r2 = refs[6:]
    x, y, _, c = coords(me[0])

    def fetch(core):
        for j in range(4):
            r1[(x - j) & 3] = other[j] if core else own[j][:8]
            for a5 in range(2):
                for k in range(2):
                    if core:
                        block = own[j][8 * a5 : 8 * a5 + 8, 2 * k + 1]
                    else:
                        block = other[j, :, 2 * a5 + k]
                    r2[(y & 1) ^ (j // 2), a5, (x - 2 * (j % 2) - k) & 3] = block

    for core in range(2):

        @pl.when(c == core)
        def _(core=core):
            fetch(core)

    order = one_hot(
        lambda lane: ((lane >> 5 ^ y) & 1) * 64
        + (lane >> 4 & 1) * 32
        + (lane >> 2 & 3) * 8
        + (lane >> 6) * 4
        + (lane & 3),
        jnp.bfloat16,
    )
    for g in range(4):
        t = r1[g].reshape(8 * P_SIZE, 128)
        hi = t.astype(jnp.bfloat16)
        lo = (t - hi.astype(jnp.float32)).astype(jnp.bfloat16)
        t = jnp.dot(hi, order, preferred_element_type=jnp.float32) + jnp.dot(
            lo, order, preferred_element_type=jnp.float32
        )
        r1[g] = t.reshape(8, 4, 16, 128)
    for r in range(16):
        t = r2[:, :, :, :, r, :].reshape(128, 128).T
        for b2 in range(2):
            row = r // 4 * 8 + b2 * 4 + r % 4
            one = r1[row // 8, row % 8].reshape(P_SIZE, 128)
            out[:, row, :] = one + t[64 * b2 : 64 * b2 + 64]


def finish(me, own, other):
    f32 = jnp.float32
    return pl.pallas_call(
        finish_kernel,
        out_shape=jax.ShapeDtypeStruct((P_SIZE, 32, 128), f32),
        in_specs=[SMEM] + [VMEM] * 5,
        out_specs=VMEM,
        scratch_shapes=[
            pltpu.VMEM((4, 8, 4, 16, 128), f32),
            pltpu.VMEM((2, 2, 4, 8, 16, 128), f32),
        ],
        compiler_params=pltpu.CompilerParams(vmem_limit_bytes=16 << 20),
        name="finish",
    )(me, *own, other)


def transposed_forward():
    m = np.zeros((128, 128), np.float32)
    for c in range(BLK):
        for d in range(BLK):
            m[c * BLK + d, d * BLK + c] = 1
            m[64 + d * BLK + c, 64 + d * BLK + c] = 1
    return m


def on_device(pairs, offsets, amplitudes, slabs):
    me = lax.axis_index(AXES)
    c = me >> 3 & 1
    core = lambda x, y, z, c: (x, y, z, c + 1)
    slabs = slabs.reshape(STEPS, 2, OWN * BLK, DEPTH)
    mine = lax.dynamic_index_in_dim(slabs, c, 0, keepdims=False)
    yours = lax.dynamic_index_in_dim(slabs, 1 - c, 0, keepdims=False)
    swapped = send(yours[0], core)
    mixed = jnp.concatenate([mine[0], swapped])
    groups = [
        [flat(x, y, z, k) for z in range(Z)]
        for x in range(X)
        for y in range(Y)
        for k in range(CORES)
    ]
    rows = lax.all_gather(mixed, AXES, axis_index_groups=groups, axis=0, tiled=True)
    cols = [
        send(mine[1], rehome),
        send(yours[1], lambda x, y, z, c: rehome(x, y, z, c + 1)),
    ]
    me = me[None]
    t = own_blocks(me, offsets, amplitudes, mixed)
    def near(n):
        return lambda x, y, z, c: (x + n * (1 - c), y + n * c, z, c)

    def far(n):
        return lambda x, y, z, c: (x + n * c, y + n * (1 - c), z, c)

    t = (
        t
        + send(t, core)
        + send(t, far(2))
        + send(t, lambda x, y, z, c: (x + 2 * (1 - c), y + 2 * c, z, 1 - c))
    )
    t = jnp.pad(t, ((0, 0), (0, DEPTH - 1024)))
    first = [jnp.concatenate(cols + [t])]
    first += [send(first[0], near(n)) for n in range(1, 4)]
    cols = jnp.stack([m[:64].reshape(8, BLK, DEPTH) for m in first])
    cols = jnp.transpose(cols, (2, 0, 1, 3)).reshape(256, DEPTH)
    second = [cols] + [send(cols, far(n)) for n in range(1, 4)]
    t = sum(m[64:, :1024] for m in first[1:]) + first[0][64:, :1024]
    t = t + cols[:16, :1024] * 0
    for n in (1, 2, 4):
        t = t + send(t, lambda x, y, z, c, n=n: (x, y, z ^ n, c))
    t = t + send(t, far(1))
    offdiag = (pairs[:, 0] != pairs[:, 1]).astype(jnp.float32)
    offdiag = jnp.broadcast_to(offdiag[:, None], (P_SIZE, 128))
    swap = jnp.asarray(transposed_forward(), jnp.bfloat16)
    keep, *give = ladder(me, offdiag, swap, t, rows, second)

    got = [pack(keep[k] + send(give[k], core)) for k in range(4)]
    for k in range(1, 4):
        got[k] = send(got[k], lambda x, y, z, c, k=k: (x + k * c, y, z + 2 * k * (1 - c), c))

    def onward(j):
        def where(x, y, z, c):
            if c == 0:
                return x + j, y, z, c
            x, y, z, c = rehome(x, y, z, c)
            return x, y ^ (j // 2), z, c

        return where

    own = [unpack(send(piece, onward(j))) for j, piece in enumerate(route(me[0], got))]
    return finish(me, own, send(split(me, own), core))


def solution(mesh):
    in_specs = (P(), P(), P(None, "vrow", "vcol"), P(None, None, ("vrow", "vcol"), None, None))
    out_specs = P(None, "vrow", "vcol")
    return jax.shard_map(
        on_device, mesh=mesh, in_specs=in_specs, out_specs=out_specs, check_vma=False
    )
```

```python
import jax
import jax.numpy as jnp
import numpy as np
from jax import lax
from jax.experimental import pallas as pl
from jax.experimental.pallas import tpu as pltpu
from jax.sharding import PartitionSpec as P

BLK = 8
P_SIZE = 64
STEPS = 2
AXES = ("vrow", "vcol")
X, Y, Z, CORES = 4, 4, 8, 2
DEPTH = 2304
OWN = 4


SMEM = pl.BlockSpec(memory_space=pltpu.SMEM)
VMEM = pl.BlockSpec(memory_space=pltpu.VMEM)
HBM = pl.BlockSpec(memory_space=pl.ANY)


def coords(me):
    return me >> 1 & 3, me >> 4 & 3, me >> 6 << 1 | me & 1, me >> 3 & 1


def flat(x, y, z, c):
    x, y, z, c = x % X, y % Y, z % Z, c % CORES
    return z // 2 << 6 | y << 4 | c << 3 | x << 1 | z % 2


def send(block, where):
    pairs = []
    for me in range(X * Y * Z * CORES):
        pairs.append((me, flat(*where(*coords(me)))))
    return lax.ppermute(block, AXES, pairs)


def rehome(x, y, z, c):
    return x, z % 2 * 2 + y % 2, z // 2 * 2 + y // 2, c


def blocks_kernel(me, offsets, amplitudes, _, out, window, sem):
    out[...] = jnp.zeros_like(out)
    for j in range(2 * STEPS):
        first, second = offsets[j // 2, j % 2], offsets[j // 2, 1 - j % 2]
        row, at_lane = first & 31, second & 127

        @pl.when(me[0] == (first >> 5 << 3 | second >> 7))
        def _(j=j, row=row, at_lane=at_lane):
            rows = pl.ds(pl.multiple_of(row & 16, 16), 16)
            copy = pltpu.make_async_copy(amplitudes.at[:, rows, :], window, sem)
            copy.start()
            copy.wait()
            block = window[...].astype(jnp.float32)
            block = jnp.where(row & 8 == 0, block[:, :8], block[:, 8:])
            lane = lax.broadcasted_iota(jnp.int32, (P_SIZE, 128), 1)
            total = jnp.zeros((P_SIZE, 128), jnp.float32)
            for r in range(BLK):
                line = jnp.where((lane >= at_lane) & (lane < at_lane + BLK), block[:, r], 0.0)
                shift = (128 + j % 2 * 64 + r * BLK - at_lane) & 127
                total = total + pltpu.roll(line, shift, 1)
            total = total.astype(jnp.bfloat16)
            for n in range(4):
                at = 128 * (j // 2 * 4 + n)
                out[:, at : at + 128] += total[16 * n : 16 * n + 16]


def own_blocks(me, offsets, amplitudes, rows):
    return pl.pallas_call(
        blocks_kernel,
        out_shape=jax.ShapeDtypeStruct((16, 1024), jnp.bfloat16),
        in_specs=[SMEM, SMEM, HBM, HBM],
        out_specs=VMEM,
        scratch_shapes=[
            pltpu.VMEM((P_SIZE, 16, 128), jnp.bfloat16),
            pltpu.SemaphoreType.DMA(()),
        ],
        compiler_params=pltpu.CompilerParams(vmem_limit_bytes=4 << 20),
        name="blocks",
    )(me, offsets, amplitudes, rows)


def one_hot(to, dtype):
    lane = lax.broadcasted_iota(jnp.int32, (128, 128), 0)
    return jnp.where(to(lane) == lax.broadcasted_iota(jnp.int32, (128, 128), 1), 1.0, 0.0).astype(
        dtype
    )


def ladder_kernel(me, offdiag, swap, blocks, a_in, *refs):
    b_in = refs[0:4]
    keep, give = refs[4], refs[5:9]
    a_all, b_all, m_all, mine, other, sems = refs[9:]
    x, y, z, c = coords(me[0])
    copies = []
    for j in range(8):
        at = (((j // 2 - (z >> 1)) & 3) * 2 + j % 2) * 64
        copies.append(
            pltpu.make_async_copy(
                a_in.at[pl.ds(64 * j, 64), :],
                a_all.at[pl.ds(pl.multiple_of(at, 64), 64), :],
                sems.at[j],
            )
        )
    for d in range(BLK):
        for j in range(4):
            copies.append(
                pltpu.make_async_copy(
                    b_in[j].at[pl.ds(32 * d, 32), :],
                    b_all.at[d, pl.ds(32 * j, 32), :],
                    sems.at[8 + d * 4 + j],
                )
            )
    for copy in copies:
        copy.start()
    for copy in copies[:8]:
        copy.wait()
    for d in range(0, BLK, 2):
        for copy in copies[8 + 4 * d : 16 + 4 * d]:
            copy.wait()
        cols = b_all[d : d + 2].reshape(256, DEPTH)
        m = lax.dot_general(
            a_all[...], cols, (((1,), (1,)), ((), ())), preferred_element_type=jnp.float32
        )
        m_all[:, d] = m[:, :128].reshape(64, BLK, 128)
        m_all[:, d + 1] = m[:, 128:].reshape(64, BLK, 128)
    parts = []
    for n in range(4):
        one, two = (blocks[:, at : at + 128] for at in (128 * n, 128 * n + 512))
        parts.append(jnp.where(c == 0, one.astype(jnp.float32), two.astype(jnp.float32)))
    t = jnp.concatenate(parts).astype(jnp.bfloat16)
    t = jnp.dot(t, swap[...], preferred_element_type=jnp.float32)
    forward, mirror = t[:, :64], t[:, 64:]
    plus = 0.5 * (forward + mirror)
    here = lax.broadcasted_iota(jnp.int32, (P_SIZE, P_SIZE), 0)
    here = here == lax.broadcasted_iota(jnp.int32, (P_SIZE, P_SIZE), 1)
    column = jnp.sum(jnp.where(here, offdiag[...], 0.0), axis=1, keepdims=True)
    minus = 0.5 * (forward - mirror) * column
    u = jnp.concatenate([plus + minus, plus - minus])
    hi = u.astype(jnp.bfloat16)
    lo = (u - hi.astype(jnp.float32)).astype(jnp.bfloat16)
    left = jnp.concatenate([hi, hi, lo], axis=1)

    def target(lane):
        near, far = lane >> 3 & 3, lane >> 5
        src_x = (x - jnp.where(c == 0, near, far)) & 3
        src_y = (y - jnp.where(c == 0, far, near)) & 3
        return (
            (src_y >> 1) * 64
            + ((src_y ^ y) & 1) * 32
            + ((lane >> 2 ^ c) & 1) * 16
            + src_x * 4
            + (lane & 3)
        )

    order = one_hot(target, jnp.bfloat16)
    for g in range(32):
        w = m_all[2 * g : 2 * g + 2].reshape(128, 128)
        hi = w.astype(jnp.bfloat16)
        lo = (w - hi.astype(jnp.float32)).astype(jnp.bfloat16)
        both = jnp.dot(
            jnp.concatenate([hi, lo]), order, preferred_element_type=jnp.float32
        ).astype(jnp.bfloat16)
        parts = []
        for n in range(2):
            hi, lo = both[64 * n : 64 * n + 64], both[128 + 64 * n : 192 + 64 * n]
            parts.append(jnp.concatenate([hi, lo, hi]))
        res = jnp.dot(left, jnp.concatenate(parts, axis=1), preferred_element_type=jnp.float32)
        kz, zl, ec, i = g // 8, g // 4 % 2, g // 2 % 2, g % 2 * 2
        at = 8 * ((1 - c) if ec else c) + 4 * zl + i
        x0, x1 = res[64:, :128], res[64:, 128:]
        top = jnp.concatenate([x0[:, :64], x1[:, :64]], axis=1)
        bottom = jnp.concatenate([x0[:, 64:], x1[:, 64:]], axis=1)
        turned = jnp.concatenate([top, bottom]).T
        kx = (kz + (z >> 1) - x) & 3
        for n in range(2):
            one = res[:64, 128 * n : 128 * n + 128].reshape(4, 16, 128)
            two = turned[64 * n : 64 * n + 64].reshape(4, 16, 128)
            mine[kz, at + n] = jnp.where(c == 0, one, two)
            other[kz, at + n] = jnp.where(c == 0, two, one)
        if g % 8 == 7:
            mine[kz, 16] = jnp.max(jnp.abs(mine[kz, :16]), axis=0)
            other[kz, 16] = jnp.max(jnp.abs(other[kz, :16]), axis=0)
            to = keep.at[jnp.where(c == 0, kz, kx)]
            pltpu.make_async_copy(mine.at[kz], to, sems.at[kz]).start()
            for k in range(4):

                @pl.when(jnp.where(c == 0, kx, kz) == k)
                def _(kz=kz, k=k):
                    pltpu.make_async_copy(other.at[kz], give[k], sems.at[4 + kz]).start()

    for kz in range(4):
        pltpu.make_async_copy(mine.at[kz], keep.at[kz], sems.at[kz]).wait()
        pltpu.make_async_copy(other.at[kz], give[kz], sems.at[4 + kz]).wait()


def ladder(me, offdiag, swap, blocks, rows, cols):
    f32, bf16 = jnp.float32, jnp.bfloat16
    return pl.pallas_call(
        ladder_kernel,
        out_shape=[jax.ShapeDtypeStruct((4, 17, 4, 16, 128), f32)]
        + [jax.ShapeDtypeStruct((17, 4, 16, 128), f32)] * 4,
        in_specs=[SMEM, VMEM, VMEM, VMEM] + [HBM] * 5,
        out_specs=[HBM] * 5,
        scratch_shapes=[
            pltpu.VMEM((512, DEPTH), bf16),
            pltpu.VMEM((BLK, 128, DEPTH), bf16),
            pltpu.VMEM((64, BLK, BLK, 128), f32),
            pltpu.VMEM((4, 17, 4, 16, 128), f32),
            pltpu.VMEM((4, 17, 4, 16, 128), f32),
            pltpu.SemaphoreType.DMA((40,)),
        ],
        compiler_params=pltpu.CompilerParams(vmem_limit_bytes=56 << 20),
        name="ladder",
    )(me, offdiag, swap, blocks, rows, *cols)


def pack(block):
    power = jnp.clip(jnp.floor(jnp.log2(block[16:])), -100.0, 100.0)
    return jnp.concatenate([block[:16] * jnp.exp2(14.0 - power), power]).astype(jnp.float16)


def unpack(block):
    block = block.astype(jnp.float32)
    return block[:16] * jnp.exp2(block[16:] - 14.0)


def route(me, got):
    x, _, z, c = coords(me)
    every = jnp.stack(got)
    out = []
    for j in range(4):
        whole = lax.dynamic_index_in_dim(every, ((z >> 1) - x - j) & 3, 0, keepdims=False)
        e, k = j // 2, j % 2 * 2
        rows = [got[k + n][:, 2 * e : 2 * e + 2] for n in range(2)]
        out.append(jnp.where(c == 0, whole, jnp.concatenate(rows, axis=1)))
    return out


def split_kernel(me, *refs):
    own, out = refs[:4], refs[4]
    c = coords(me[0])[3]

    @pl.when(c == 0)
    def _():
        for j in range(4):
            out[j] = own[j][8:]

    @pl.when(c == 1)
    def _():
        for j in range(4):
            for a5 in range(2):
                for k in range(2):
                    out[j, :, 2 * a5 + k] = own[j][8 * a5 : 8 * a5 + 8, 2 * k]


def split(me, own):
    return pl.pallas_call(
        split_kernel,
        out_shape=jax.ShapeDtypeStruct((4, 8, 4, 16, 128), own[0].dtype),
        in_specs=[SMEM] + [VMEM] * 4,
        out_specs=VMEM,
        compiler_params=pltpu.CompilerParams(vmem_limit_bytes=10 << 20),
        name="split",
    )(me, *own)


def finish_kernel(me, *refs):
    own, other, out = refs[:4], refs[4], refs[5]
    r1, r2 = refs[6:]
    x, y, _, c = coords(me[0])

    def fetch(core):
        for j in range(4):
            r1[(x - j) & 3] = other[j] if core else own[j][:8]
            for a5 in range(2):
                for k in range(2):
                    if core:
                        block = own[j][8 * a5 : 8 * a5 + 8, 2 * k + 1]
                    else:
                        block = other[j, :, 2 * a5 + k]
                    r2[(y & 1) ^ (j // 2), a5, (x - 2 * (j % 2) - k) & 3] = block

    for core in range(2):

        @pl.when(c == core)
        def _(core=core):
            fetch(core)

    order = one_hot(
        lambda lane: ((lane >> 5 ^ y) & 1) * 64
        + (lane >> 4 & 1) * 32
        + (lane >> 2 & 3) * 8
        + (lane >> 6) * 4
        + (lane & 3),
        jnp.bfloat16,
    )
    for g in range(4):
        t = r1[g].reshape(8 * P_SIZE, 128)
        hi = t.astype(jnp.bfloat16)
        lo = (t - hi.astype(jnp.float32)).astype(jnp.bfloat16)
        t = jnp.dot(hi, order, preferred_element_type=jnp.float32) + jnp.dot(
            lo, order, preferred_element_type=jnp.float32
        )
        r1[g] = t.reshape(8, 4, 16, 128)
    for r in range(16):
        t = r2[:, :, :, :, r, :].reshape(128, 128).T
        for b2 in range(2):
            row = r // 4 * 8 + b2 * 4 + r % 4
            one = r1[row // 8, row % 8].reshape(P_SIZE, 128)
            out[:, row, :] = one + t[64 * b2 : 64 * b2 + 64]


def finish(me, own, other):
    f32 = jnp.float32
    return pl.pallas_call(
        finish_kernel,
        out_shape=jax.ShapeDtypeStruct((P_SIZE, 32, 128), f32),
        in_specs=[SMEM] + [VMEM] * 5,
        out_specs=VMEM,
        scratch_shapes=[
            pltpu.VMEM((4, 8, 4, 16, 128), f32),
            pltpu.VMEM((2, 2, 4, 8, 16, 128), f32),
        ],
        compiler_params=pltpu.CompilerParams(vmem_limit_bytes=16 << 20),
        name="finish",
    )(me, *own, other)


def transposed_forward():
    m = np.zeros((128, 128), np.float32)
    for c in range(BLK):
        for d in range(BLK):
            m[c * BLK + d, d * BLK + c] = 1
            m[64 + d * BLK + c, 64 + d * BLK + c] = 1
    return m


def on_device(pairs, offsets, amplitudes, slabs):
    me = lax.axis_index(AXES)
    c = me >> 3 & 1
    core = lambda x, y, z, c: (x, y, z, c + 1)
    slabs = slabs.reshape(STEPS, 2, OWN * BLK, DEPTH)
    mine = lax.dynamic_index_in_dim(slabs, c, 0, keepdims=False)
    yours = lax.dynamic_index_in_dim(slabs, 1 - c, 0, keepdims=False)
    swapped = send(yours[0], core)
    mixed = jnp.concatenate([mine[0], swapped])
    groups = [
        [flat(x, y, z, k) for z in range(Z)]
        for x in range(X)
        for y in range(Y)
        for k in range(CORES)
    ]
    rows = lax.all_gather(mixed, AXES, axis_index_groups=groups, axis=0, tiled=True)
    cols = [
        send(mine[1], rehome),
        send(yours[1], lambda x, y, z, c: rehome(x, y, z, c + 1)),
    ]
    me = me[None]
    t = own_blocks(me, offsets, amplitudes, mixed)
    def near(n):
        return lambda x, y, z, c: (x + n * (1 - c), y + n * c, z, c)

    def far(n):
        return lambda x, y, z, c: (x + n * c, y + n * (1 - c), z, c)

    t = (
        t
        + send(t, core)
        + send(t, far(2))
        + send(t, lambda x, y, z, c: (x + 2 * (1 - c), y + 2 * c, z, 1 - c))
    )
    t = jnp.pad(t, ((0, 0), (0, DEPTH - 1024)))
    first = [jnp.concatenate(cols + [t])]
    first += [send(first[0], near(n)) for n in range(1, 4)]
    cols = jnp.stack([m[:64].reshape(8, BLK, DEPTH) for m in first])
    cols = jnp.transpose(cols, (2, 0, 1, 3)).reshape(256, DEPTH)
    second = [cols] + [send(cols, far(n)) for n in range(1, 4)]
    t = sum(m[64:, :1024] for m in first[1:]) + first[0][64:, :1024]
    t = t + cols[:16, :1024] * 0
    for n in (1, 2, 4):
        t = t + send(t, lambda x, y, z, c, n=n: (x, y, z ^ n, c))
    t = t + send(t, far(1))
    offdiag = (pairs[:, 0] != pairs[:, 1]).astype(jnp.float32)
    offdiag = offdiag[None, :]
    swap = jnp.asarray(transposed_forward(), jnp.bfloat16)
    keep, *give = ladder(me, offdiag, swap, t, rows, second)

    got = [pack(keep[k] + send(give[k], core)) for k in range(4)]
    for k in range(1, 4):
        got[k] = send(got[k], lambda x, y, z, c, k=k: (x + k * c, y, z + 2 * k * (1 - c), c))

    def onward(j):
        def where(x, y, z, c):
            if c == 0:
                return x + j, y, z, c
            x, y, z, c = rehome(x, y, z, c)
            return x, y ^ (j // 2), z, c

        return where

    own = [unpack(send(piece, onward(j))) for j, piece in enumerate(route(me[0], got))]
    return finish(me, own, send(split(me, own), core))


def solution(mesh):
    in_specs = (P(), P(), P(None, "vrow", "vcol"), P(None, None, ("vrow", "vcol"), None, None))
    out_specs = P(None, "vrow", "vcol")
    return jax.shard_map(
        on_device, mesh=mesh, in_specs=in_specs, out_specs=out_specs, check_vma=False
    )
```
